32 devices in a mesh: dp: 4 (over y, x), expert: 8 (over z, core).
Axes of the slice: x: 2, y: 2, z: 4, core: 2. Of those that a mesh axis runs over, the one named last changes fastest.
Arguments:
- tokens: bfloat16 [4096, 2048], P(('dp', 'expert')), may hold values from -6 to 6
- expert_ids: int32 [4096, 1], P(('dp', 'expert')), may hold values from 0 to 7; in each aligned block of 128 rows (0 to 127, 128 to 255, ...) at most 20 rows name the same one
- route_weight: float32 [4096, 1], P(('dp', 'expert')), may hold values from 0.1 to 1
- cotangent: bfloat16 [4096, 2048], P(('dp', 'expert')), may hold values from -0.59765625 to 0.59765625
- w_gate: bfloat16 [8192, 2048], P('expert', 'dp'), may hold values from -0.125 to 0.125
- w_up: bfloat16 [8192, 2048], P('expert', 'dp'), may hold values from -0.125 to 0.125
- w_down: bfloat16 [8192, 2048], P('expert', 'dp'), may hold values from -0.1875 to 0.1875
Outputs:
- layer_out: bfloat16 [4096, 2048], P(('dp', 'expert'))
- token_grad: bfloat16 [4096, 2048], P(('dp', 'expert'))
- gate_grad: bfloat16 [8192, 2048], P('expert', 'dp')
- up_grad: bfloat16 [8192, 2048], P('expert', 'dp')
- down_grad: bfloat16 [8192, 2048], P('expert', 'dp')
The draws below stay inside these ranges and needn't reach their ends.
Inputs may be any that keep to these rules, and one draw needn't show every extreme that they name: `expert_ids`: among the 128 rows of one device, at most 20 name the same expert.
All inputs are finite; a program needn't handle non-finite values.
Results may differ from the reference program's by a relative error of at most 0.018.
Values may be sent and summed in bfloat16 or wider, within the bound.
A program may use at most 64 MiB of HBM per device.

```python
import math
import jax
import jax.numpy as jnp
import numpy as np
from jax import lax

D = 2048
H = 1024
EXPERTS = 8
TOK_DEV = 128
CAP = 20
GROUP = 1
HS = 1024
TOKENS = 4096
N_DP = 4
N_EXPERT = 8


def block_levels(rng, shape, shards, smallest, largest):
    gain, own = 1.0, jax.random.fold_in(rng, 6)
    for dim, shards_of in shards:
        draws = jnp.exp(jax.random.uniform(jax.random.fold_in(own, dim), (shards_of,), jnp.float32, smallest / len(shards), largest / len(shards)))
        gain = gain * jnp.repeat(draws, shape[dim] // shards_of).reshape([-1 if axis == dim else 1 for axis in range(len(shape))])
    return gain


def routed_block(stream_key, own, number, rows, number_of, top, limit, skew):
    ranking = jax.random.permutation(stream_key, number_of)
    crowded, common = load_shares(number_of, rows * top, limit, skew, True), load_shares(number_of, rows * top, limit, skew, False)
    places = jnp.arange(number_of)

    def named(lengths, offset_by):
        used = int((lengths > 0).sum())
        fixed = max(1, used // 4)
        moved = fixed + (places - fixed + offset_by * (used - fixed)) % max(1, number_of - fixed)
        return jnp.zeros((number_of,), jnp.int32).at[ranking[jnp.where(places < fixed, places, moved)]].set(jnp.asarray(lengths, jnp.int32))

    lengths = jnp.where(number % 4 == 0, named(crowded, number // 4), named(common, number - number // 4 - 1))
    mixed = jax.random.permutation(jax.random.fold_in(own, 3), number_of)
    donor, receiver = mixed[0:number_of // 2 * 2:2], mixed[1:number_of // 2 * 2:2]
    slack = jnp.minimum(lengths[donor] - 1, limit - lengths[receiver]) // 2
    slack = jnp.where((donor == ranking[0]) | (receiver == ranking[0]) | (lengths[receiver] == 0), 0, jnp.maximum(slack, 0))
    moved = jax.random.randint(jax.random.fold_in(own, 4), (number_of // 2,), 0, 1 << 20) % (slack + 1)
    lengths = lengths.at[donor].add(-moved).at[receiver].add(moved)
    labels = jnp.searchsorted(jnp.cumsum(lengths), jnp.arange(rows * top), side="right").astype(jnp.int32)
    grid = labels.reshape(top, rows).T
    grid = grid[jax.random.permutation(jax.random.fold_in(own, 1), rows)]
    offset_by = jax.random.randint(jax.random.fold_in(own, 2), (rows, 1), 0, top)
    return jnp.take_along_axis(grid, (jnp.arange(top)[None, :] + offset_by) % top, axis=1)


def load_shares(count, total, limit, skew, full):
    weights = [(1 << 20) // math.isqrt(grade ** skew) + 1 for grade in range(1, count + 1)]
    largest = limit if full else min(limit, max(-(-total // count), total * weights[0] // sum(weights)))
    least = 1 if total - largest >= count - 1 else 0
    counts, surplus = [largest] + [least] * (count - 1), total - largest - least * (count - 1)
    while surplus > 0:
        movable = [i for i in range(1, count) if counts[i] < largest] or [i for i in range(1, count) if counts[i] < limit]
        whole, left = sum([weights[i] for i in movable]), surplus
        for i in movable:
            addition = min(limit - counts[i], max(1, left * weights[i] // whole), surplus)
            counts[i] = counts[i] + addition
            surplus = surplus - addition
    return np.array(counts)


def noise(key, dims, spread, most, split=(), held_as=jnp.bfloat16):
    values = spread * jax.random.normal(key, dims, jnp.float32)
    if split:
        values = values * block_levels(key, dims, split, -0.22, 0.18)
    return jnp.clip(values, -most, most).astype(held_as)


def setup_inputs(seed: int = 0) -> dict:
    arg_keys = jax.random.split(jax.random.key(seed), 8)
    tokens = noise(arg_keys[0], (TOKENS, D), 1.0, 6.0, ((0, 32),))
    expert_ids_keys = jax.random.split(jax.random.fold_in(arg_keys[1], 1), TOKENS // TOK_DEV)
    expert_ids_turns = jax.random.permutation(jax.random.fold_in(arg_keys[1], 3), TOKENS // TOK_DEV)
    expert_ids = jax.vmap(lambda own, number: routed_block(jax.random.fold_in(arg_keys[1], 2), own, number, TOK_DEV, EXPERTS, 1, CAP, 2))(expert_ids_keys, expert_ids_turns).reshape((TOKENS, 1))
    route_weight = jnp.clip(jnp.exp(math.log(1.0) - 2.3025851 * jax.random.uniform(arg_keys[2], (TOKENS, 1), jnp.float32) ** block_levels(arg_keys[2], (TOKENS, 1), ((0, 32),), -0.2, 0.2)), 0.1, 1.0)
    cotangent = noise(arg_keys[3], (TOKENS, D), 0.1, 0.59765625, ((0, 32),))
    w_gate = noise(arg_keys[4], (EXPERTS * H, D), D ** -0.5, 0.125, ((0, 8), (1, 4)))
    w_up = noise(arg_keys[5], (EXPERTS * H, D), D ** -0.5, 0.125, ((0, 8), (1, 4)))
    w_down = noise(arg_keys[6], (EXPERTS * H, D), H ** -0.5, 0.1875, ((0, 8), (1, 4)))
    return {"tokens": tokens, "expert_ids": expert_ids, "route_weight": route_weight, "cotangent": cotangent, "w_gate": w_gate, "w_up": w_up, "w_down": w_down}


def rounded_sum(partials):
    return jnp.sum(lax.optimization_barrier(partials.astype(jnp.bfloat16)).astype(jnp.float32), axis=0)


def reference(tokens, expert_ids, route_weight, cotangent, w_gate, w_up, w_down):
    features = tokens.shape[1]
    sources = N_EXPERT
    blocks = N_DP * N_EXPERT
    chosen = expert_ids[:, 0].reshape(blocks, TOK_DEV)
    onehot = (chosen[:, :, None] == jnp.arange(EXPERTS, dtype=jnp.int32)[None, None, :]).astype(jnp.int32)
    before = jnp.cumsum(onehot, axis=1) - onehot
    slot_index = (chosen * CAP + jnp.sum(before * onehot, axis=2)).astype(jnp.int32)
    slot_owner = jnp.full((blocks, EXPERTS * CAP), TOK_DEV, dtype=jnp.int32)
    block_ids = jnp.arange(blocks, dtype=jnp.int32)[:, None]
    token_ids = jnp.broadcast_to(jnp.arange(TOK_DEV, dtype=jnp.int32)[None, :], (blocks, TOK_DEV))
    slot_owner = slot_owner.at[block_ids, slot_index].set(token_ids)
    scaled = (route_weight * cotangent.astype(jnp.float32)).astype(jnp.bfloat16)
    source_ids = jnp.repeat(jnp.arange(sources, dtype=jnp.int32), CAP)
    zero_rows = jnp.zeros((sources * CAP, features), jnp.bfloat16)

    def one_expert(row_block, expert_pos):
        owners = lax.dynamic_slice(slot_owner, (row_block * sources, expert_pos * CAP), (sources, CAP)).reshape(-1)
        occupied = owners < TOK_DEV
        token_index = jnp.where(occupied, (row_block * sources + source_ids) * TOK_DEV + owners, 0).astype(jnp.int32)
        token_rows = jnp.where(occupied[:, None], tokens[token_index], zero_rows)
        grad_rows = jnp.where(occupied[:, None], scaled[token_index], zero_rows)
        weight_rows = jnp.where(occupied, route_weight[token_index, 0], jnp.zeros_like(route_weight[token_index, 0]))
        start = (expert_pos * H).astype(jnp.int32)
        gate_rows = lax.dynamic_slice_in_dim(w_gate, start, H, 0)
        up_rows = lax.dynamic_slice_in_dim(w_up, start, H, 0)
        down_rows = lax.dynamic_slice_in_dim(w_down, start, H, 0)
        gate_pre = jnp.dot(token_rows, gate_rows.T, preferred_element_type=jnp.float32)
        up_pre = jnp.dot(token_rows, up_rows.T, preferred_element_type=jnp.float32)
        gate_sigmoid = jax.nn.sigmoid(gate_pre)
        gate_silu = gate_pre * gate_sigmoid
        hidden = (gate_silu * up_pre).astype(jnp.bfloat16)
        count = hidden.shape[0]
        down_split = down_rows.astype(jnp.float32).reshape(GROUP, HS, features)
        gate_split = gate_rows.astype(jnp.float32).reshape(GROUP, HS, features)
        up_split = up_rows.astype(jnp.float32).reshape(GROUP, HS, features)
        out_terms = jnp.einsum("ngh,ghd->gnd", hidden.astype(jnp.float32).reshape(count, GROUP, HS), down_split)
        out_slots = (weight_rows[:, None] * rounded_sum(out_terms)).astype(jnp.bfloat16)
        hidden_grad = jnp.dot(grad_rows, down_rows.T, preferred_element_type=jnp.float32)
        gate_grad_pre = (hidden_grad * up_pre * (gate_sigmoid * (1.0 + gate_pre * (1.0 - gate_sigmoid)))).astype(jnp.bfloat16)
        up_grad_pre = (hidden_grad * gate_silu).astype(jnp.bfloat16)
        input_terms = jnp.einsum("ngh,ghd->gnd", gate_grad_pre.astype(jnp.float32).reshape(count, GROUP, HS), gate_split)
        input_terms = input_terms + jnp.einsum("ngh,ghd->gnd", up_grad_pre.astype(jnp.float32).reshape(count, GROUP, HS), up_split)
        back_slots = rounded_sum(input_terms).astype(jnp.bfloat16)
        gate_term = jnp.dot(gate_grad_pre.T, token_rows, preferred_element_type=jnp.float32).astype(jnp.bfloat16)
        up_term = jnp.dot(up_grad_pre.T, token_rows, preferred_element_type=jnp.float32).astype(jnp.bfloat16)
        down_term = jnp.dot(hidden.T, grad_rows, preferred_element_type=jnp.float32).astype(jnp.bfloat16)
        return out_slots, back_slots, gate_term, up_term, down_term

    def per_block(totals, row_block):
        results = lax.map(lambda expert_pos: one_expert(row_block, expert_pos), jnp.arange(EXPERTS, dtype=jnp.int32))
        out_slots, back_slots, gate_term, up_term, down_term = results
        gate_add = lax.optimization_barrier(gate_term).astype(jnp.float32).reshape(EXPERTS * H, features)
        up_add = lax.optimization_barrier(up_term).astype(jnp.float32).reshape(EXPERTS * H, features)
        down_add = lax.optimization_barrier(down_term).astype(jnp.float32).reshape(EXPERTS * H, features)
        return (totals[0] + gate_add, totals[1] + up_add, totals[2] + down_add), (out_slots, back_slots)

    zero_grads = jnp.zeros((EXPERTS * H, features), jnp.float32)
    totals, stacked = lax.scan(per_block, (zero_grads, zero_grads, zero_grads), jnp.arange(N_DP, dtype=jnp.int32))
    out_all, back_all = stacked
    slot_pos = slot_index - chosen * CAP
    flat = ((block_ids // sources) * EXPERTS + chosen) * (sources * CAP) + (block_ids % sources) * CAP + slot_pos
    flat = flat.reshape(-1).astype(jnp.int32)
    layer_out = out_all.reshape(-1, features)[flat]
    token_grad = back_all.reshape(-1, features)[flat]
    return (layer_out, token_grad, totals[0].astype(jnp.bfloat16), totals[1].astype(jnp.bfloat16), totals[2].astype(jnp.bfloat16))
```

```python
import jax
import jax.numpy as jnp
from jax import lax
from jax.sharding import PartitionSpec as P

EXPERTS = 8
CAP = 20
BOTH = ("dp", "expert")


def spread(slots, cols, group_size):
    n_dp = lax.axis_size("dp")
    pieces = slots.reshape(EXPERTS, CAP, n_dp, cols).transpose(2, 0, 1, 3)
    sending = jnp.repeat(pieces, group_size, axis=1).reshape(-1, CAP, cols)
    arrived = lax.all_to_all(sending, BOTH, split_axis=0, concat_axis=0, tiled=True)
    return arrived.reshape(-1, cols)


def bring_back(rows, cols, group_size):
    n_dp = lax.axis_size("dp")
    sending = rows.astype(jnp.bfloat16).reshape(-1, CAP, cols)
    arrived = lax.all_to_all(sending, BOTH, split_axis=0, concat_axis=0, tiled=True)
    pieces = arrived.reshape(n_dp, EXPERTS, group_size, CAP, cols)
    if group_size > 1:
        pieces = jnp.sum(pieces.astype(jnp.float32), axis=2).astype(jnp.bfloat16)
    else:
        pieces = pieces[:, :, 0]
    return pieces.transpose(1, 2, 0, 3).reshape(EXPERTS * CAP, n_dp * cols)


def scatter_sum(partial):
    return lax.psum_scatter(
        partial.astype(jnp.bfloat16), "dp", scatter_dimension=0, tiled=True
    ).astype(jnp.float32)


def local(tokens, expert_ids, route_weight, cotangent, w_gate, w_up, w_down):
    cols = w_gate.shape[1]
    group_size = lax.axis_size("expert") // EXPERTS
    chosen = expert_ids[:, 0]
    onehot = (chosen[:, None] == jnp.arange(EXPERTS, dtype=jnp.int32)[None, :]).astype(jnp.int32)
    before = jnp.cumsum(onehot, axis=0) - onehot
    slot_index = chosen * CAP + jnp.sum(before * onehot, axis=1)
    placing = (jnp.arange(EXPERTS * CAP, dtype=jnp.int32)[:, None] == slot_index[None, :]).astype(
        jnp.bfloat16
    )
    scaled = (route_weight * cotangent.astype(jnp.float32)).astype(jnp.bfloat16)
    token_slots = jnp.dot(placing, tokens, preferred_element_type=jnp.float32).astype(jnp.bfloat16)
    grad_slots = jnp.dot(placing, scaled, preferred_element_type=jnp.float32).astype(jnp.bfloat16)
    token_rows = spread(token_slots, cols, group_size)
    gate_pre = scatter_sum(
        jnp.einsum("nd,hd->nh", token_rows, w_gate, preferred_element_type=jnp.float32)
    )
    up_pre = scatter_sum(
        jnp.einsum("nd,hd->nh", token_rows, w_up, preferred_element_type=jnp.float32)
    )
    grad_rows = spread(grad_slots, cols, group_size)
    hidden_grad = scatter_sum(
        jnp.einsum("nd,hd->nh", grad_rows, w_down, preferred_element_type=jnp.float32)
    )
    gate_sigmoid = jax.nn.sigmoid(gate_pre)
    gate_silu = gate_pre * gate_sigmoid
    hidden = (gate_silu * up_pre).astype(jnp.bfloat16)
    hidden = lax.all_gather(hidden, "dp", axis=0, tiled=True)
    gate_grad_pre = (
        hidden_grad * up_pre * (gate_sigmoid * (1.0 + gate_pre * (1.0 - gate_sigmoid)))
    ).astype(jnp.bfloat16)
    gate_grad_pre = lax.all_gather(gate_grad_pre, "dp", axis=0, tiled=True)
    up_grad_pre = (hidden_grad * gate_silu).astype(jnp.bfloat16)
    up_grad_pre = lax.all_gather(up_grad_pre, "dp", axis=0, tiled=True)
    out_slots = bring_back(
        jnp.dot(hidden, w_down, preferred_element_type=jnp.float32), cols, group_size
    )
    input_term = jnp.dot(gate_grad_pre, w_gate, preferred_element_type=jnp.float32) + jnp.dot(
        up_grad_pre, w_up, preferred_element_type=jnp.float32
    )
    back_slots = bring_back(input_term, cols, group_size)
    picked = jnp.einsum("st,sd->td", placing, out_slots, preferred_element_type=jnp.float32)
    layer_out = (route_weight * picked).astype(jnp.bfloat16)
    token_grad = jnp.einsum(
        "st,sd->td", placing, back_slots, preferred_element_type=jnp.float32
    ).astype(jnp.bfloat16)
    gate_grad = jnp.einsum("nh,nd->hd", gate_grad_pre, token_rows, preferred_element_type=jnp.float32)
    up_grad = jnp.einsum("nh,nd->hd", up_grad_pre, token_rows, preferred_element_type=jnp.float32)
    down_grad = jnp.einsum("nh,nd->hd", hidden, grad_rows, preferred_element_type=jnp.float32)
    return (
        layer_out,
        token_grad,
        gate_grad.astype(jnp.bfloat16),
        up_grad.astype(jnp.bfloat16),
        down_grad.astype(jnp.bfloat16),
    )


def solution(mesh):
    return jax.shard_map(
        local,
        mesh=mesh,
        in_specs=(
            P(BOTH, None),
            P(BOTH, None),
            P(BOTH, None),
            P(BOTH, None),
            P("expert", "dp"),
            P("expert", "dp"),
            P("expert", "dp"),
        ),
        out_specs=(
            P(BOTH, None),
            P(BOTH, None),
            P("expert", "dp"),
            P("expert", "dp"),
            P("expert", "dp"),
        ),
        check_vma=False,
    )
```

```python
import functools

import jax
import jax.numpy as jnp
import numpy as np
from jax import lax
from jax.experimental import pallas as pl
from jax.experimental.pallas import tpu as pltpu
from jax.sharding import PartitionSpec as P

EXPERTS = 8
CAP = 20
BOTH = ("dp", "expert")
LANES = 128
MESH = pl.DeviceIdType.MESH


def spread(slots, cols, group_size):
    n_dp = lax.axis_size("dp")
    pieces = slots.reshape(EXPERTS, CAP, n_dp, cols).transpose(2, 0, 1, 3)
    sending = jnp.repeat(pieces, group_size, axis=1).reshape(-1, CAP, cols)
    arrived = lax.all_to_all(sending, BOTH, split_axis=0, concat_axis=0, tiled=True)
    return arrived.reshape(-1, cols)


def bring_back(rows, cols, group_size):
    n_dp = lax.axis_size("dp")
    sending = rows.astype(jnp.bfloat16).reshape(-1, CAP, cols)
    arrived = lax.all_to_all(sending, BOTH, split_axis=0, concat_axis=0, tiled=True)
    pieces = arrived.reshape(n_dp, EXPERTS, group_size, CAP, cols)
    if group_size > 1:
        pieces = jnp.sum(pieces.astype(jnp.float32), axis=2).astype(jnp.bfloat16)
    else:
        pieces = pieces[:, :, 0]
    return pieces.transpose(1, 2, 0, 3).reshape(EXPERTS * CAP, n_dp * cols)


def scatter_sum(partial):
    return lax.psum_scatter(
        partial.astype(jnp.bfloat16), "dp", scatter_dimension=0, tiled=True
    ).astype(jnp.float32)


def local(tokens, expert_ids, route_weight, cotangent, w_gate, w_up, w_down):
    cols = w_gate.shape[1]
    group_size = lax.axis_size("expert") // EXPERTS
    chosen = expert_ids[:, 0]
    onehot = (chosen[:, None] == jnp.arange(EXPERTS, dtype=jnp.int32)[None, :]).astype(jnp.int32)
    before = jnp.cumsum(onehot, axis=0) - onehot
    slot_index = chosen * CAP + jnp.sum(before * onehot, axis=1)
    placing = (jnp.arange(EXPERTS * CAP, dtype=jnp.int32)[:, None] == slot_index[None, :]).astype(
        jnp.bfloat16
    )
    scaled = (route_weight * cotangent.astype(jnp.float32)).astype(jnp.bfloat16)
    token_slots = jnp.dot(placing, tokens, preferred_element_type=jnp.float32).astype(jnp.bfloat16)
    grad_slots = jnp.dot(placing, scaled, preferred_element_type=jnp.float32).astype(jnp.bfloat16)
    token_rows = spread(token_slots, cols, group_size)
    gate_pre = scatter_sum(
        jnp.einsum("nd,hd->nh", token_rows, w_gate, preferred_element_type=jnp.float32)
    )
    up_pre = scatter_sum(
        jnp.einsum("nd,hd->nh", token_rows, w_up, preferred_element_type=jnp.float32)
    )
    grad_rows = spread(grad_slots, cols, group_size)
    hidden_grad = scatter_sum(
        jnp.einsum("nd,hd->nh", grad_rows, w_down, preferred_element_type=jnp.float32)
    )
    gate_sigmoid = jax.nn.sigmoid(gate_pre)
    gate_silu = gate_pre * gate_sigmoid
    hidden = (gate_silu * up_pre).astype(jnp.bfloat16)
    hidden = lax.all_gather(hidden, "dp", axis=0, tiled=True)
    gate_grad_pre = (
        hidden_grad * up_pre * (gate_sigmoid * (1.0 + gate_pre * (1.0 - gate_sigmoid)))
    ).astype(jnp.bfloat16)
    gate_grad_pre = lax.all_gather(gate_grad_pre, "dp", axis=0, tiled=True)
    up_grad_pre = (hidden_grad * gate_silu).astype(jnp.bfloat16)
    up_grad_pre = lax.all_gather(up_grad_pre, "dp", axis=0, tiled=True)
    out_slots = bring_back(
        jnp.dot(hidden, w_down, preferred_element_type=jnp.float32), cols, group_size
    )
    input_term = jnp.dot(gate_grad_pre, w_gate, preferred_element_type=jnp.float32) + jnp.dot(
        up_grad_pre, w_up, preferred_element_type=jnp.float32
    )
    back_slots = bring_back(input_term, cols, group_size)
    picked = jnp.einsum("st,sd->td", placing, out_slots, preferred_element_type=jnp.float32)
    layer_out = (route_weight * picked).astype(jnp.bfloat16)
    token_grad = jnp.einsum(
        "st,sd->td", placing, back_slots, preferred_element_type=jnp.float32
    ).astype(jnp.bfloat16)
    gate_grad = jnp.einsum("nh,nd->hd", gate_grad_pre, token_rows, preferred_element_type=jnp.float32)
    up_grad = jnp.einsum("nh,nd->hd", up_grad_pre, token_rows, preferred_element_type=jnp.float32)
    down_grad = jnp.einsum("nh,nd->hd", hidden, grad_rows, preferred_element_type=jnp.float32)
    return (
        layer_out,
        token_grad,
        gate_grad.astype(jnp.bfloat16),
        up_grad.astype(jnp.bfloat16),
        down_grad.astype(jnp.bfloat16),
    )


def dot_nt(a, b):
    return lax.dot_general(a, b, (((1,), (1,)), ((), ())), preferred_element_type=jnp.float32)


def dot_tn(a, b):
    return lax.dot_general(a, b, (((0,), (0,)), ((), ())), preferred_element_type=jnp.float32)


def dot_nn(a, b):
    return jnp.dot(a, b, preferred_element_type=jnp.float32)


def fused_kernel(
    n_dp,
    ids_ref,
    weight_ref,
    row_key_ref,
    lane_key_ref,
    tokens_ref,
    cot_ref,
    w_gate_ref,
    w_up_ref,
    w_down_ref,
    layer_out_ref,
    token_grad_ref,
    gate_grad_ref,
    up_grad_ref,
    down_grad_ref,
    slots,
    rows_in,
    raw,
    rows,
    partial,
    own_partial,
    summed_in,
    hidden_all,
    back_out,
    back_in,
    final,
    big,
    pick,
    spread_send,
    spread_recv,
    piece_send,
    piece_recv,
    sum_send,
    sum_recv,
    hid_send,
    hid_recv,
    ret_send,
    ret_recv,
    fin_send,
    fin_recv,
):
    n_ex = EXPERTS
    n_tok = tokens_ref.shape[0]
    cols = w_gate_ref.shape[1]
    width = w_gate_ref.shape[0]
    chunks = cols // LANES
    block = chunks * CAP
    group_rows = n_ex * CAP
    d = lax.axis_index("dp")
    e = lax.axis_index("expert")

    def dp_at(k):
        return lax.rem(d + k + n_dp, n_dp)

    def ex_at(k):
        return lax.rem(e + k + n_ex, n_ex)

    def copy(src, dst, send_sem, recv_sem, to_dp, to_ex):
        return pltpu.make_async_remote_copy(
            src_ref=src,
            dst_ref=dst,
            send_sem=send_sem,
            recv_sem=recv_sem,
            device_id=(to_dp, to_ex),
            device_id_type=MESH,
        )

    barrier = pltpu.get_barrier_semaphore()
    for k in range(1, n_ex):
        pl.semaphore_signal(barrier, inc=1, device_id=(d, ex_at(k)), device_id_type=MESH)
    for k in range(1, n_dp):
        pl.semaphore_signal(barrier, inc=1, device_id=(dp_at(k), e), device_id_type=MESH)

    ids = ids_ref[...]
    onehot = ids == lax.broadcasted_iota(jnp.int32, (n_ex, n_tok), 0)
    onehot_f = onehot.astype(jnp.float32)
    earlier = (
        lax.broadcasted_iota(jnp.int32, (n_tok, n_tok), 0)
        < lax.broadcasted_iota(jnp.int32, (n_tok, n_tok), 1)
    ).astype(jnp.bfloat16)
    before = dot_nn(onehot_f.astype(jnp.bfloat16), earlier)
    place = jnp.sum(onehot_f * before, axis=0, keepdims=True).astype(jnp.int32)
    slot = ids * CAP + place
    row_key = row_key_ref[...]
    for c in range(chunks):
        big[:, c * n_tok : (c + 1) * n_tok] = (
            (row_key == slot + c * group_rows).astype(jnp.float32).astype(jnp.bfloat16)
        )
    lane_key = lane_key_ref[...]
    for c in range(chunks):
        want = lax.broadcasted_iota(jnp.int32, (group_rows, 1), 0) + c * group_rows
        pick[c] = (lane_key == want).astype(jnp.float32).astype(jnp.bfloat16)

    started = []

    def spread(a, source):
        for j in range(n_dp):
            stack = jnp.concatenate(
                [
                    source[:, j * cols + c * LANES : j * cols + (c + 1) * LANES]
                    for c in range(chunks)
                ],
                axis=0,
            )
            placed = dot_nn(big[...], stack).astype(jnp.bfloat16)
            slots[a, :, :, j * LANES : (j + 1) * LANES] = placed.reshape(n_ex, block, LANES)

    def send_spread(a):
        for k in range(1, n_ex):
            to = ex_at(k)
            cp = copy(
                slots.at[a, to], rows_in.at[a, e], spread_send.at[a, k], spread_recv.at[a, k], d, to
            )
            cp.start()
            started.append(cp)
        rows_in[a, e] = slots[a, e]

    spread(0, tokens_ref[...])
    pl.semaphore_wait(barrier, n_ex - 1 + n_dp - 1)
    send_spread(0)
    spread(1, (weight_ref[...] * cot_ref[...].astype(jnp.float32)).astype(jnp.bfloat16))
    send_spread(1)

    def forward(a):
        for k in range(n_ex):
            source = ex_at(-k)
            if k > 0:
                copy(
                    rows_in.at[a, source],
                    rows_in.at[a, source],
                    spread_send.at[a, k],
                    spread_recv.at[a, k],
                    d,
                    source,
                ).wait_recv()
            for kd in range(1, n_dp):
                to = dp_at(kd)
                cp = copy(
                    rows_in.at[a, source, :, pl.ds(pl.multiple_of(to * LANES, LANES), LANES)],
                    raw.at[a, kd, source],
                    piece_send.at[a, kd, k],
                    piece_recv.at[a, kd, k],
                    to,
                    e,
                )
                cp.start()
                started.append(cp)
        raw[a, 0] = rows_in[a, :, :, pl.ds(pl.multiple_of(d * LANES, LANES), LANES)]

    def arrange(a, kd):
        if kd > 0:
            for k in range(n_ex):
                source = lax.rem(e - k + n_ex, n_ex)
                copy(
                    raw.at[a, kd, source],
                    raw.at[a, kd, source],
                    piece_send.at[a, kd, k],
                    piece_recv.at[a, kd, k],
                    dp_at(-kd),
                    e,
                ).wait_recv()
        arrived = raw[a, kd].reshape(n_ex * block, LANES)
        for c in range(chunks):
            rows[a, kd, :, c * LANES : (c + 1) * LANES] = dot_nn(pick[c], arrived).astype(
                jnp.bfloat16
            )

    def multiply(m, a, kd, w_ref):
        value = dot_nt(rows[a, kd], w_ref[...])
        if kd == 0:
            own_partial[m] = value
            return
        partial[m, kd - 1] = value.astype(jnp.bfloat16)
        cp = copy(
            partial.at[m, kd - 1],
            summed_in.at[m, kd - 1],
            sum_send.at[m, kd],
            sum_recv.at[m, kd],
            dp_at(-kd),
            e,
        )
        cp.start()
        started.append(cp)

    forward(0)
    for kd in range(n_dp):
        arrange(0, kd)
        multiply(0, 0, kd, w_gate_ref)
        multiply(1, 0, kd, w_up_ref)
    forward(1)
    for kd in range(n_dp):
        arrange(1, kd)
        multiply(2, 1, kd, w_down_ref)

    def total(m):
        for kd in range(1, n_dp):
            copy(
                summed_in.at[m, kd - 1],
                summed_in.at[m, kd - 1],
                sum_send.at[m, kd],
                sum_recv.at[m, kd],
                dp_at(kd),
                e,
            ).wait_recv()
        value = own_partial[m]
        for kd in range(1, n_dp):
            value = value + summed_in[m, kd - 1].astype(jnp.float32)
        return value

    def share(m, value):
        hidden_all[m, 0] = value
        for kd in range(1, n_dp):
            cp = copy(
                hidden_all.at[m, 0],
                hidden_all.at[m, kd],
                hid_send.at[m, kd],
                hid_recv.at[m, kd],
                dp_at(kd),
                e,
            )
            cp.start()
            started.append(cp)

    gate_pre = total(0)
    sigmoid = 1.0 / (1.0 + jnp.exp(-gate_pre))
    silu = gate_pre * sigmoid
    own_partial[0] = silu
    up_pre = total(1)
    share(0, (silu * up_pre).astype(jnp.bfloat16))
    own_partial[1] = up_pre * (sigmoid * (1.0 + gate_pre * (1.0 - sigmoid)))
    hidden_grad = total(2)
    share(1, (hidden_grad * own_partial[1]).astype(jnp.bfloat16))
    share(2, (hidden_grad * own_partial[0]).astype(jnp.bfloat16))

    def wait_hidden(m, kd):
        if kd > 0:
            copy(
                hidden_all.at[m, kd],
                hidden_all.at[m, kd],
                hid_send.at[m, kd],
                hid_recv.at[m, kd],
                dp_at(-kd),
                e,
            ).wait_recv()

    def send_back(b, kd, value):
        value = value.astype(jnp.bfloat16)
        back = dot_tn(pick[0], value[:, :LANES])
        for c in range(1, chunks):
            back = back + dot_tn(pick[c], value[:, c * LANES : (c + 1) * LANES])
        back = back.astype(jnp.bfloat16).reshape(n_ex, block, LANES)
        if kd == 0:
            back_in[b, 0] = back
            return
        back_out[b, kd - 1] = back
        cp = copy(
            back_out.at[b, kd - 1],
            back_in.at[b, kd],
            ret_send.at[b, kd],
            ret_recv.at[b, kd],
            dp_at(-kd),
            e,
        )
        cp.start()
        started.append(cp)

    def finish_send(b, kd):
        if kd > 0:
            copy(
                back_in.at[b, kd],
                back_in.at[b, kd],
                ret_send.at[b, kd],
                ret_recv.at[b, kd],
                dp_at(kd),
                e,
            ).wait_recv()
        j = dp_at(kd)
        for k in range(1, n_ex):
            to = ex_at(k)
            cp = copy(
                back_in.at[b, kd, to],
                final.at[b, j, e],
                fin_send.at[b, kd, k],
                fin_recv.at[b, kd, k],
                d,
                to,
            )
            cp.start()
            started.append(cp)
        final[b, j, e] = back_in[b, kd, e]

    for kd in range(n_dp):
        wait_hidden(0, kd)
        send_back(0, kd, dot_nn(hidden_all[0, kd], w_down_ref[...]))
    for kd in range(n_dp):
        finish_send(0, kd)
    for kd in range(n_dp):
        wait_hidden(1, kd)
        wait_hidden(2, kd)
        send_back(
            1,
            kd,
            dot_nn(hidden_all[1, kd], w_gate_ref[...]) + dot_nn(hidden_all[2, kd], w_up_ref[...]),
        )
    for kd in range(n_dp):
        finish_send(1, kd)

    tile = 256 if width % 256 == 0 else width
    for m, a, out_ref in ((0, 1, down_grad_ref), (1, 0, gate_grad_ref), (2, 0, up_grad_ref)):
        right = rows[a].reshape(n_dp * group_rows, cols)
        for t in range(width // tile):
            left = hidden_all[m, :, :, t * tile : (t + 1) * tile].reshape(n_dp * group_rows, tile)
            out_ref[t * tile : (t + 1) * tile, :] = dot_tn(left, right).astype(jnp.bfloat16)

    def place_back(b, out_ref):
        for kd in range(n_dp):
            for k in range(1, n_ex):
                source = ex_at(-k)
                copy(
                    final.at[b, dp_at(kd), source],
                    final.at[b, dp_at(kd), source],
                    fin_send.at[b, kd, k],
                    fin_recv.at[b, kd, k],
                    d,
                    source,
                ).wait_recv()
        for j in range(n_dp):
            value = dot_tn(big[...], final[b, j].reshape(n_ex * block, LANES))
            for c in range(chunks):
                piece = value[c * n_tok : (c + 1) * n_tok]
                if b == 0:
                    piece = weight_ref[...] * piece
                out_ref[:, j * cols + c * LANES : j * cols + (c + 1) * LANES] = piece.astype(
                    jnp.bfloat16
                )

    place_back(0, layer_out_ref)
    place_back(1, token_grad_ref)
    for cp in started:
        cp.wait_send()


def local_fused(tokens, expert_ids, route_weight, cotangent, w_gate, w_up, w_down):
    n_dp = lax.axis_size("dp")
    n_ex = lax.axis_size("expert")
    n_tok, features = tokens.shape
    width, cols = w_gate.shape
    chunks = cols // LANES
    block = chunks * CAP
    group_rows = n_ex * CAP
    at = np.arange(n_ex * block)
    key = (at // block) * CAP + at % CAP + ((at % block) // CAP) * group_rows
    key = key.astype(np.int32)
    bf16 = jnp.bfloat16
    vmem = pl.BlockSpec(memory_space=pltpu.VMEM)
    dma = pltpu.SemaphoreType.DMA
    return pl.pallas_call(
        functools.partial(fused_kernel, n_dp),
        out_shape=(
            jax.ShapeDtypeStruct((n_tok, features), bf16),
            jax.ShapeDtypeStruct((n_tok, features), bf16),
            jax.ShapeDtypeStruct((width, cols), bf16),
            jax.ShapeDtypeStruct((width, cols), bf16),
            jax.ShapeDtypeStruct((width, cols), bf16),
        ),
        in_specs=[vmem] * 9,
        out_specs=(vmem,) * 5,
        scratch_shapes=[
            pltpu.VMEM((2, n_ex, block, n_dp * LANES), bf16),
            pltpu.VMEM((2, n_ex, block, n_dp * LANES), bf16),
            pltpu.VMEM((2, n_dp, n_ex, block, LANES), bf16),
            pltpu.VMEM((2, n_dp, group_rows, cols), bf16),
            pltpu.VMEM((3, n_dp - 1, group_rows, width), bf16),
            pltpu.VMEM((3, group_rows, width), jnp.float32),
            pltpu.VMEM((3, n_dp - 1, group_rows, width), bf16),
            pltpu.VMEM((3, n_dp, group_rows, width), bf16),
            pltpu.VMEM((2, n_dp - 1, n_ex, block, LANES), bf16),
            pltpu.VMEM((2, n_dp, n_ex, block, LANES), bf16),
            pltpu.VMEM((2, n_dp, n_ex, block, LANES), bf16),
            pltpu.VMEM((n_ex * block, chunks * n_tok), bf16),
            pltpu.VMEM((chunks, group_rows, n_ex * block), bf16),
            dma((2, n_ex)),
            dma((2, n_ex)),
            dma((2, n_dp, n_ex)),
            dma((2, n_dp, n_ex)),
            dma((3, n_dp)),
            dma((3, n_dp)),
            dma((3, n_dp)),
            dma((3, n_dp)),
            dma((2, n_dp)),
            dma((2, n_dp)),
            dma((2, n_dp, n_ex)),
            dma((2, n_dp, n_ex)),
        ],
        compiler_params=pltpu.CompilerParams(
            collective_id=0, has_side_effects=True, vmem_limit_bytes=56 * 1024 * 1024
        ),
        cost_estimate=pl.CostEstimate(
            flops=18 * n_dp * group_rows * width * cols,
            bytes_accessed=12 * width * cols + 8 * n_tok * features,
            transcendentals=group_rows * width,
        ),
    )(
        expert_ids.reshape(1, n_tok),
        route_weight,
        jnp.asarray(key)[:, None],
        jnp.asarray(key)[None, :],
        tokens,
        cotangent,
        w_gate,
        w_up,
        w_down,
    )


def solution(mesh):
    one_block = mesh.shape["expert"] == EXPERTS
    return jax.shard_map(
        local_fused if one_block else local,
        mesh=mesh,
        in_specs=(
            P(BOTH, None),
            P(BOTH, None),
            P(BOTH, None),
            P(BOTH, None),
            P("expert", "dp"),
            P("expert", "dp"),
            P("expert", "dp"),
        ),
        out_specs=(
            P(BOTH, None),
            P(BOTH, None),
            P("expert", "dp"),
            P("expert", "dp"),
            P("expert", "dp"),
        ),
        check_vma=False,
    )
```

```python
import functools

import jax
import jax.numpy as jnp
import numpy as np
from jax import lax
from jax.experimental import pallas as pl
from jax.experimental.pallas import tpu as pltpu
from jax.sharding import PartitionSpec as P

EXPERTS = 8
CAP = 20
BOTH = ("dp", "expert")
LANES = 128
MESH = pl.DeviceIdType.MESH


def spread(slots, cols, group_size):
    n_dp = lax.axis_size("dp")
    pieces = slots.reshape(EXPERTS, CAP, n_dp, cols).transpose(2, 0, 1, 3)
    sending = jnp.repeat(pieces, group_size, axis=1).reshape(-1, CAP, cols)
    arrived = lax.all_to_all(sending, BOTH, split_axis=0, concat_axis=0, tiled=True)
    return arrived.reshape(-1, cols)


def bring_back(rows, cols, group_size):
    n_dp = lax.axis_size("dp")
    sending = rows.astype(jnp.bfloat16).reshape(-1, CAP, cols)
    arrived = lax.all_to_all(sending, BOTH, split_axis=0, concat_axis=0, tiled=True)
    pieces = arrived.reshape(n_dp, EXPERTS, group_size, CAP, cols)
    if group_size > 1:
        pieces = jnp.sum(pieces.astype(jnp.float32), axis=2).astype(jnp.bfloat16)
    else:
        pieces = pieces[:, :, 0]
    return pieces.transpose(1, 2, 0, 3).reshape(EXPERTS * CAP, n_dp * cols)


def scatter_sum(partial):
    return lax.psum_scatter(
        partial.astype(jnp.bfloat16), "dp", scatter_dimension=0, tiled=True
    ).astype(jnp.float32)


def local(tokens, expert_ids, route_weight, cotangent, w_gate, w_up, w_down):
    cols = w_gate.shape[1]
    group_size = lax.axis_size("expert") // EXPERTS
    chosen = expert_ids[:, 0]
    onehot = (chosen[:, None] == jnp.arange(EXPERTS, dtype=jnp.int32)[None, :]).astype(jnp.int32)
    before = jnp.cumsum(onehot, axis=0) - onehot
    slot_index = chosen * CAP + jnp.sum(before * onehot, axis=1)
    placing = (jnp.arange(EXPERTS * CAP, dtype=jnp.int32)[:, None] == slot_index[None, :]).astype(
        jnp.bfloat16
    )
    scaled = (route_weight * cotangent.astype(jnp.float32)).astype(jnp.bfloat16)
    token_slots = jnp.dot(placing, tokens, preferred_element_type=jnp.float32).astype(jnp.bfloat16)
    grad_slots = jnp.dot(placing, scaled, preferred_element_type=jnp.float32).astype(jnp.bfloat16)
    token_rows = spread(token_slots, cols, group_size)
    gate_pre = scatter_sum(
        jnp.einsum("nd,hd->nh", token_rows, w_gate, preferred_element_type=jnp.float32)
    )
    up_pre = scatter_sum(
        jnp.einsum("nd,hd->nh", token_rows, w_up, preferred_element_type=jnp.float32)
    )
    grad_rows = spread(grad_slots, cols, group_size)
    hidden_grad = scatter_sum(
        jnp.einsum("nd,hd->nh", grad_rows, w_down, preferred_element_type=jnp.float32)
    )
    gate_sigmoid = jax.nn.sigmoid(gate_pre)
    gate_silu = gate_pre * gate_sigmoid
    hidden = (gate_silu * up_pre).astype(jnp.bfloat16)
    hidden = lax.all_gather(hidden, "dp", axis=0, tiled=True)
    gate_grad_pre = (
        hidden_grad * up_pre * (gate_sigmoid * (1.0 + gate_pre * (1.0 - gate_sigmoid)))
    ).astype(jnp.bfloat16)
    gate_grad_pre = lax.all_gather(gate_grad_pre, "dp", axis=0, tiled=True)
    up_grad_pre = (hidden_grad * gate_silu).astype(jnp.bfloat16)
    up_grad_pre = lax.all_gather(up_grad_pre, "dp", axis=0, tiled=True)
    out_slots = bring_back(
        jnp.dot(hidden, w_down, preferred_element_type=jnp.float32), cols, group_size
    )
    input_term = jnp.dot(gate_grad_pre, w_gate, preferred_element_type=jnp.float32) + jnp.dot(
        up_grad_pre, w_up, preferred_element_type=jnp.float32
    )
    back_slots = bring_back(input_term, cols, group_size)
    picked = jnp.einsum("st,sd->td", placing, out_slots, preferred_element_type=jnp.float32)
    layer_out = (route_weight * picked).astype(jnp.bfloat16)
    token_grad = jnp.einsum(
        "st,sd->td", placing, back_slots, preferred_element_type=jnp.float32
    ).astype(jnp.bfloat16)
    gate_grad = jnp.einsum("nh,nd->hd", gate_grad_pre, token_rows, preferred_element_type=jnp.float32)
    up_grad = jnp.einsum("nh,nd->hd", up_grad_pre, token_rows, preferred_element_type=jnp.float32)
    down_grad = jnp.einsum("nh,nd->hd", hidden, grad_rows, preferred_element_type=jnp.float32)
    return (
        layer_out,
        token_grad,
        gate_grad.astype(jnp.bfloat16),
        up_grad.astype(jnp.bfloat16),
        down_grad.astype(jnp.bfloat16),
    )


def dot_nt(a, b):
    return lax.dot_general(a, b, (((1,), (1,)), ((), ())), preferred_element_type=jnp.float32)


def dot_tn(a, b):
    return lax.dot_general(a, b, (((0,), (0,)), ((), ())), preferred_element_type=jnp.float32)


def dot_nn(a, b):
    return jnp.dot(a, b, preferred_element_type=jnp.float32)


def fused_kernel(
    n_dp,
    ids_ref,
    weight_ref,
    row_key_ref,
    lane_key_ref,
    tokens_ref,
    cot_ref,
    w_gate_ref,
    w_up_ref,
    w_down_ref,
    final,
    big,
    gate_grad_ref,
    up_grad_ref,
    down_grad_ref,
    slots,
    rows_in,
    raw,
    rows,
    partial,
    own_partial,
    summed_in,
    relayed,
    hidden_all,
    back_out,
    back_in,
    pick,
    spread_send,
    spread_recv,
    piece_send,
    piece_recv,
    sum_send,
    sum_recv,
    hid_send,
    hid_recv,
    ret_send,
    ret_recv,
    fin_send,
    fin_recv,
):
    n_ex = EXPERTS
    n_tok = tokens_ref.shape[0]
    cols = w_gate_ref.shape[1]
    width = w_gate_ref.shape[0]
    chunks = cols // LANES
    block = chunks * CAP
    group_rows = n_ex * CAP
    half = group_rows // 2
    d = lax.axis_index("dp")
    e = lax.axis_index("expert")

    across_x = d + 1 - 2 * lax.rem(d, 2)
    peers = (d, across_x, lax.rem(d + 2, 4), 3 - d)

    def dp_at(k):
        return peers[k]

    def ex_at(k):
        return lax.rem(e + k + n_ex, n_ex)

    def copy(src, dst, send_sem, recv_sem, to_dp, to_ex):
        return pltpu.make_async_remote_copy(
            src_ref=src,
            dst_ref=dst,
            send_sem=send_sem,
            recv_sem=recv_sem,
            device_id=(to_dp, to_ex),
            device_id_type=MESH,
        )

    barrier = pltpu.get_barrier_semaphore()
    for k in range(1, n_ex):
        pl.semaphore_signal(barrier, inc=1, device_id=(d, ex_at(k)), device_id_type=MESH)
    for k in range(1, n_dp):
        pl.semaphore_signal(barrier, inc=1, device_id=(dp_at(k), e), device_id_type=MESH)

    ids = ids_ref[...]
    onehot = ids == lax.broadcasted_iota(jnp.int32, (n_ex, n_tok), 0)
    onehot_f = onehot.astype(jnp.float32)
    earlier = (
        lax.broadcasted_iota(jnp.int32, (n_tok, n_tok), 0)
        < lax.broadcasted_iota(jnp.int32, (n_tok, n_tok), 1)
    ).astype(jnp.bfloat16)
    before = dot_nn(onehot_f.astype(jnp.bfloat16), earlier)
    place = jnp.sum(onehot_f * before, axis=0, keepdims=True).astype(jnp.int32)
    slot = ids * CAP + place
    row_key = row_key_ref[...]
    for c in range(chunks):
        big[:, c * n_tok : (c + 1) * n_tok] = (
            (row_key == slot + c * group_rows).astype(jnp.float32).astype(jnp.bfloat16)
        )
    lane_key = lane_key_ref[...]
    for c in range(chunks):
        want = lax.broadcasted_iota(jnp.int32, (group_rows, 1), 0) + c * group_rows
        pick[c] = (lane_key == want).astype(jnp.float32).astype(jnp.bfloat16)

    started = []

    def spread(a, source):
        for j in range(n_dp):
            stack = jnp.concatenate(
                [
                    source[:, j * cols + c * LANES : j * cols + (c + 1) * LANES]
                    for c in range(chunks)
                ],
                axis=0,
            )
            placed = dot_nn(big[...], stack).astype(jnp.bfloat16)
            slots[a, :, :, j * LANES : (j + 1) * LANES] = placed.reshape(n_ex, block, LANES)

    def send_spread(a):
        for k in range(1, n_ex):
            to = ex_at(k)
            cp = copy(
                slots.at[a, to], rows_in.at[a, e], spread_send.at[a, k], spread_recv.at[a, k], d, to
            )
            cp.start()
            started.append(cp)
        rows_in[a, e] = slots[a, e]

    spread(0, tokens_ref[...])
    pl.semaphore_wait(barrier, n_ex - 1 + n_dp - 1)
    send_spread(0)
    spread(1, (weight_ref[...] * cot_ref[...].astype(jnp.float32)).astype(jnp.bfloat16))
    send_spread(1)

    def forward(a):
        for k in range(n_ex):
            source = ex_at(-k)
            if k > 0:
                copy(
                    rows_in.at[a, source],
                    rows_in.at[a, source],
                    spread_send.at[a, k],
                    spread_recv.at[a, k],
                    d,
                    source,
                ).wait_recv()
            for kd in range(1, n_dp):
                to = dp_at(kd)
                cp = copy(
                    rows_in.at[a, source, :, pl.ds(pl.multiple_of(to * LANES, LANES), LANES)],
                    raw.at[a, kd, source],
                    piece_send.at[a, kd, k],
                    piece_recv.at[a, kd, k],
                    to,
                    e,
                )
                cp.start()
                started.append(cp)
        raw[a, 0] = rows_in[a, :, :, pl.ds(pl.multiple_of(d * LANES, LANES), LANES)]

    def arrange(a, kd):
        if kd > 0:
            for k in range(n_ex):
                source = lax.rem(e - k + n_ex, n_ex)
                copy(
                    raw.at[a, kd, source],
                    raw.at[a, kd, source],
                    piece_send.at[a, kd, k],
                    piece_recv.at[a, kd, k],
                    dp_at(kd),
                    e,
                ).wait_recv()
        arrived = raw[a, kd].reshape(n_ex * block, LANES)
        for c in range(chunks):
            rows[a, kd, :, c * LANES : (c + 1) * LANES] = dot_nn(pick[c], arrived).astype(
                jnp.bfloat16
            )

    upper, lower = pl.ds(0, half), pl.ds(half, half)

    def send_sum(m, i, src, to):
        cp = copy(src, summed_in.at[m, i], sum_send.at[m, i], sum_recv.at[m, i], dp_at(to), e)
        cp.start()
        started.append(cp)

    def wait_sum(m, i, source):
        dst = summed_in.at[m, i]
        copy(dst, dst, sum_send.at[m, i], sum_recv.at[m, i], dp_at(source), e).wait_recv()

    def multiply(m, a, kd, w_ref):
        value = dot_nt(rows[a, kd], w_ref[...])
        if kd == 0:
            own_partial[m] = value
            return
        partial[m, kd - 1] = value.astype(jnp.bfloat16)
        if kd == 1:
            send_sum(m, 0, partial.at[m, 0, upper], 1)
        elif kd == 2:
            send_sum(m, 2, partial.at[m, 1, lower], 2)
        else:
            send_sum(m, 1, partial.at[m, 2, upper], 1)
            send_sum(m, 3, partial.at[m, 2, lower], 2)

    def relay_sum(m):
        wait_sum(m, 1, 1)
        relayed[m, 0] = (
            partial[m, 1, :half].astype(jnp.float32) + summed_in[m, 1].astype(jnp.float32)
        ).astype(jnp.bfloat16)
        send_sum(m, 4, relayed.at[m, 0], 2)
        wait_sum(m, 3, 2)
        relayed[m, 1] = (
            partial[m, 0, half:].astype(jnp.float32) + summed_in[m, 3].astype(jnp.float32)
        ).astype(jnp.bfloat16)
        send_sum(m, 5, relayed.at[m, 1], 1)

    def total(m):
        wait_sum(m, 0, 1)
        wait_sum(m, 2, 2)
        wait_sum(m, 4, 2)
        wait_sum(m, 5, 1)
        own = own_partial[m]
        top = own[:half] + (
            summed_in[m, 0].astype(jnp.float32) + summed_in[m, 4].astype(jnp.float32)
        )
        bottom = own[half:] + (
            summed_in[m, 2].astype(jnp.float32) + summed_in[m, 5].astype(jnp.float32)
        )
        return jnp.concatenate([top, bottom], axis=0)

    forward(0)
    for kd in range(n_dp):
        arrange(0, kd)
        multiply(0, 0, kd, w_gate_ref)
        multiply(1, 0, kd, w_up_ref)
    forward(1)
    relay_sum(0)
    relay_sum(1)
    for kd in range(n_dp):
        arrange(1, kd)
        multiply(2, 1, kd, w_down_ref)

    def send_hidden(m, kd, src, dst, to):
        cp = copy(src, dst, hid_send.at[m, kd], hid_recv.at[m, kd], dp_at(to), e)
        cp.start()
        started.append(cp)

    def await_hidden(m, kd, dst, source):
        copy(dst, dst, hid_send.at[m, kd], hid_recv.at[m, kd], dp_at(source), e).wait_recv()

    def share(m, value):
        hidden_all[m, 0] = value
        for kd in (1, 2):
            send_hidden(m, kd, hidden_all.at[m, 0], hidden_all.at[m, kd], kd)

    def relay_hidden(m):
        await_hidden(m, 1, hidden_all.at[m, 1], 1)
        send_hidden(m, 3, hidden_all.at[m, 1, lower], hidden_all.at[m, 3, lower], 2)
        await_hidden(m, 2, hidden_all.at[m, 2], 2)
        send_hidden(m, 0, hidden_all.at[m, 2, upper], hidden_all.at[m, 3, upper], 1)

    def last_hidden(m):
        await_hidden(m, 3, hidden_all.at[m, 3, lower], 2)
        await_hidden(m, 0, hidden_all.at[m, 3, upper], 1)

    gate_pre = total(0)
    sigmoid = 1.0 / (1.0 + jnp.exp(-gate_pre))
    silu = gate_pre * sigmoid
    own_partial[0] = silu
    up_pre = total(1)
    share(0, (silu * up_pre).astype(jnp.bfloat16))
    own_partial[1] = up_pre * (sigmoid * (1.0 + gate_pre * (1.0 - sigmoid)))
    relay_sum(2)
    hidden_grad = total(2)
    share(1, (hidden_grad * own_partial[1]).astype(jnp.bfloat16))
    share(2, (hidden_grad * own_partial[0]).astype(jnp.bfloat16))

    def send_back(b, kd, value):
        value = value.astype(jnp.bfloat16)
        back = dot_tn(pick[0], value[:, :LANES])
        for c in range(1, chunks):
            back = back + dot_tn(pick[c], value[:, c * LANES : (c + 1) * LANES])
        back = back.astype(jnp.bfloat16).reshape(n_ex, block, LANES)
        if kd == 0:
            back_in[b, 0] = back
            return
        back_out[b, kd - 1] = back
        cp = copy(
            back_out.at[b, kd - 1],
            back_in.at[b, kd],
            ret_send.at[b, kd],
            ret_recv.at[b, kd],
            dp_at(kd),
            e,
        )
        cp.start()
        started.append(cp)

    def finish_send(b, kd):
        if kd > 0:
            copy(
                back_in.at[b, kd],
                back_in.at[b, kd],
                ret_send.at[b, kd],
                ret_recv.at[b, kd],
                dp_at(kd),
                e,
            ).wait_recv()
        j = dp_at(kd)
        for k in range(1, n_ex):
            to = ex_at(k)
            cp = copy(
                back_in.at[b, kd, to],
                final.at[b, j, e],
                fin_send.at[b, kd, k],
                fin_recv.at[b, kd, k],
                d,
                to,
            )
            cp.start()
            started.append(cp)
        final[b, j, e] = back_in[b, kd, e]

    def output(kd):
        send_back(0, kd, dot_nn(hidden_all[0, kd], w_down_ref[...]))

    def input_grad(kd):
        send_back(
            1,
            kd,
            dot_nn(hidden_all[1, kd], w_gate_ref[...]) + dot_nn(hidden_all[2, kd], w_up_ref[...]),
        )

    relay_hidden(0)
    for kd in (1, 2, 0):
        output(kd)
    relay_hidden(1)
    relay_hidden(2)
    last_hidden(0)
    output(3)
    for kd in (1, 2, 0):
        input_grad(kd)
    finish_send(0, 0)
    finish_send(0, 1)
    finish_send(0, 2)
    last_hidden(1)
    last_hidden(2)
    input_grad(3)
    finish_send(1, 0)
    finish_send(0, 3)
    finish_send(1, 1)
    finish_send(1, 2)
    finish_send(1, 3)

    tile = 256 if width % 256 == 0 else width
    for m, a, out_ref in ((0, 1, down_grad_ref), (1, 0, gate_grad_ref), (2, 0, up_grad_ref)):
        right = rows[a].reshape(n_dp * group_rows, cols)
        for t in range(width // tile):
            left = hidden_all[m, :, :, t * tile : (t + 1) * tile].reshape(n_dp * group_rows, tile)
            out_ref[t * tile : (t + 1) * tile, :] = dot_tn(left, right).astype(jnp.bfloat16)

    for b in range(2):
        for kd in range(n_dp):
            for k in range(1, n_ex):
                source = ex_at(-k)
                copy(
                    final.at[b, dp_at(kd), source],
                    final.at[b, dp_at(kd), source],
                    fin_send.at[b, kd, k],
                    fin_recv.at[b, kd, k],
                    d,
                    source,
                ).wait_recv()
    for cp in started:
        cp.wait_send()


def finish_kernel(
    weight_ref,
    big_ref,
    final_ref,
    gate_in,
    up_in,
    down_in,
    layer_out_ref,
    token_grad_ref,
    gate_out,
    up_out,
    down_out,
    sems,
):
    copies = [
        pltpu.make_async_copy(src, dst, sems.at[i])
        for i, (src, dst) in enumerate(((gate_in, gate_out), (up_in, up_out), (down_in, down_out)))
    ]
    for cp in copies:
        cp.start()
    n_tok = weight_ref.shape[0]
    n_dp = final_ref.shape[1]
    chunks = big_ref.shape[1] // n_tok
    cols = chunks * LANES
    for b, out_ref in ((0, layer_out_ref), (1, token_grad_ref)):
        for j in range(n_dp):
            value = dot_tn(big_ref[...], final_ref[b, j].reshape(big_ref.shape[0], LANES))
            for c in range(chunks):
                piece = value[c * n_tok : (c + 1) * n_tok]
                if b == 0:
                    piece = weight_ref[...] * piece
                out_ref[:, j * cols + c * LANES : j * cols + (c + 1) * LANES] = piece.astype(
                    jnp.bfloat16
                )
    for cp in copies:
        cp.wait()


def local_fused(tokens, expert_ids, route_weight, cotangent, w_gate, w_up, w_down):
    n_dp = lax.axis_size("dp")
    n_ex = lax.axis_size("expert")
    n_tok, features = tokens.shape
    width, cols = w_gate.shape
    chunks = cols // LANES
    block = chunks * CAP
    group_rows = n_ex * CAP
    at = np.arange(n_ex * block)
    key = (at // block) * CAP + at % CAP + ((at % block) // CAP) * group_rows
    key = key.astype(np.int32)
    bf16 = jnp.bfloat16
    vmem = pl.BlockSpec(memory_space=pltpu.VMEM)
    dma = pltpu.SemaphoreType.DMA
    vmem_limit = 56 * 1024 * 1024
    weight_struct = jax.ShapeDtypeStruct((width, cols), bf16)
    token_struct = jax.ShapeDtypeStruct((n_tok, features), bf16)
    final, big, gate_grad, up_grad, down_grad = pl.pallas_call(
        functools.partial(fused_kernel, n_dp),
        out_shape=(
            jax.ShapeDtypeStruct((2, n_dp, n_ex, block, LANES), bf16),
            jax.ShapeDtypeStruct((n_ex * block, chunks * n_tok), bf16),
            weight_struct,
            weight_struct,
            weight_struct,
        ),
        in_specs=[vmem] * 9,
        out_specs=(vmem,) * 5,
        scratch_shapes=[
            pltpu.VMEM((2, n_ex, block, n_dp * LANES), bf16),
            pltpu.VMEM((2, n_ex, block, n_dp * LANES), bf16),
            pltpu.VMEM((2, n_dp, n_ex, block, LANES), bf16),
            pltpu.VMEM((2, n_dp, group_rows, cols), bf16),
            pltpu.VMEM((3, n_dp - 1, group_rows, width), bf16),
            pltpu.VMEM((3, group_rows, width), jnp.float32),
            pltpu.VMEM((3, 6, group_rows // 2, width), bf16),
            pltpu.VMEM((3, 2, group_rows // 2, width), bf16),
            pltpu.VMEM((3, n_dp, group_rows, width), bf16),
            pltpu.VMEM((2, n_dp - 1, n_ex, block, LANES), bf16),
            pltpu.VMEM((2, n_dp, n_ex, block, LANES), bf16),
            pltpu.VMEM((chunks, group_rows, n_ex * block), bf16),
            dma((2, n_ex)),
            dma((2, n_ex)),
            dma((2, n_dp, n_ex)),
            dma((2, n_dp, n_ex)),
            dma((3, 6)),
            dma((3, 6)),
            dma((3, n_dp)),
            dma((3, n_dp)),
            dma((2, n_dp)),
            dma((2, n_dp)),
            dma((2, n_dp, n_ex)),
            dma((2, n_dp, n_ex)),
        ],
        compiler_params=pltpu.CompilerParams(
            collective_id=0, has_side_effects=True, vmem_limit_bytes=vmem_limit
        ),
        cost_estimate=pl.CostEstimate(
            flops=18 * n_dp * group_rows * width * cols,
            bytes_accessed=12 * width * cols + 8 * n_tok * features,
            transcendentals=group_rows * width,
        ),
    )(
        expert_ids.reshape(1, n_tok),
        route_weight,
        jnp.asarray(key)[:, None],
        jnp.asarray(key)[None, :],
        tokens,
        cotangent,
        w_gate,
        w_up,
        w_down,
    )
    hbm = pl.BlockSpec(memory_space=pl.ANY)
    return pl.pallas_call(
        finish_kernel,
        out_shape=(token_struct, token_struct, weight_struct, weight_struct, weight_struct),
        in_specs=[vmem] * 3 + [hbm] * 3,
        out_specs=(vmem,) * 2 + (hbm,) * 3,
        scratch_shapes=[dma((3,))],
        compiler_params=pltpu.CompilerParams(vmem_limit_bytes=vmem_limit),
    )(route_weight, big, final, gate_grad, up_grad, down_grad)


def solution(mesh):
    one_block = mesh.shape["expert"] == EXPERTS and mesh.shape["dp"] == 4
    return jax.shard_map(
        local_fused if one_block else local,
        mesh=mesh,
        in_specs=(
            P(BOTH, None),
            P(BOTH, None),
            P(BOTH, None),
            P(BOTH, None),
            P("expert", "dp"),
            P("expert", "dp"),
            P("expert", "dp"),
        ),
        out_specs=(
            P(BOTH, None),
            P(BOTH, None),
            P("expert", "dp"),
            P("expert", "dp"),
            P("expert", "dp"),
        ),
        check_vma=False,
    )
```

```python
import functools

import jax
import jax.numpy as jnp
import numpy as np
from jax import lax
from jax.experimental import pallas as pl
from jax.experimental.pallas import tpu as pltpu
from jax.sharding import PartitionSpec as P

EXPERTS = 8
CAP = 20
BOTH = ("dp", "expert")
LANES = 128
MESH = pl.DeviceIdType.MESH


def spread(slots, cols, group_size):
    n_dp = lax.axis_size("dp")
    pieces = slots.reshape(EXPERTS, CAP, n_dp, cols).transpose(2, 0, 1, 3)
    sending = jnp.repeat(pieces, group_size, axis=1).reshape(-1, CAP, cols)
    arrived = lax.all_to_all(sending, BOTH, split_axis=0, concat_axis=0, tiled=True)
    return arrived.reshape(-1, cols)


def bring_back(rows, cols, group_size):
    n_dp = lax.axis_size("dp")
    sending = rows.astype(jnp.bfloat16).reshape(-1, CAP, cols)
    arrived = lax.all_to_all(sending, BOTH, split_axis=0, concat_axis=0, tiled=True)
    pieces = arrived.reshape(n_dp, EXPERTS, group_size, CAP, cols)
    if group_size > 1:
        pieces = jnp.sum(pieces.astype(jnp.float32), axis=2).astype(jnp.bfloat16)
    else:
        pieces = pieces[:, :, 0]
    return pieces.transpose(1, 2, 0, 3).reshape(EXPERTS * CAP, n_dp * cols)


def scatter_sum(partial):
    return lax.psum_scatter(
        partial.astype(jnp.bfloat16), "dp", scatter_dimension=0, tiled=True
    ).astype(jnp.float32)


def local(tokens, expert_ids, route_weight, cotangent, w_gate, w_up, w_down):
    cols = w_gate.shape[1]
    group_size = lax.axis_size("expert") // EXPERTS
    chosen = expert_ids[:, 0]
    onehot = (chosen[:, None] == jnp.arange(EXPERTS, dtype=jnp.int32)[None, :]).astype(jnp.int32)
    before = jnp.cumsum(onehot, axis=0) - onehot
    slot_index = chosen * CAP + jnp.sum(before * onehot, axis=1)
    placing = (jnp.arange(EXPERTS * CAP, dtype=jnp.int32)[:, None] == slot_index[None, :]).astype(
        jnp.bfloat16
    )
    scaled = (route_weight * cotangent.astype(jnp.float32)).astype(jnp.bfloat16)
    token_slots = jnp.dot(placing, tokens, preferred_element_type=jnp.float32).astype(jnp.bfloat16)
    grad_slots = jnp.dot(placing, scaled, preferred_element_type=jnp.float32).astype(jnp.bfloat16)
    token_rows = spread(token_slots, cols, group_size)
    gate_pre = scatter_sum(
        jnp.einsum("nd,hd->nh", token_rows, w_gate, preferred_element_type=jnp.float32)
    )
    up_pre = scatter_sum(
        jnp.einsum("nd,hd->nh", token_rows, w_up, preferred_element_type=jnp.float32)
    )
    grad_rows = spread(grad_slots, cols, group_size)
    hidden_grad = scatter_sum(
        jnp.einsum("nd,hd->nh", grad_rows, w_down, preferred_element_type=jnp.float32)
    )
    gate_sigmoid = jax.nn.sigmoid(gate_pre)
    gate_silu = gate_pre * gate_sigmoid
    hidden = (gate_silu * up_pre).astype(jnp.bfloat16)
    hidden = lax.all_gather(hidden, "dp", axis=0, tiled=True)
    gate_grad_pre = (
        hidden_grad * up_pre * (gate_sigmoid * (1.0 + gate_pre * (1.0 - gate_sigmoid)))
    ).astype(jnp.bfloat16)
    gate_grad_pre = lax.all_gather(gate_grad_pre, "dp", axis=0, tiled=True)
    up_grad_pre = (hidden_grad * gate_silu).astype(jnp.bfloat16)
    up_grad_pre = lax.all_gather(up_grad_pre, "dp", axis=0, tiled=True)
    out_slots = bring_back(
        jnp.dot(hidden, w_down, preferred_element_type=jnp.float32), cols, group_size
    )
    input_term = jnp.dot(gate_grad_pre, w_gate, preferred_element_type=jnp.float32) + jnp.dot(
        up_grad_pre, w_up, preferred_element_type=jnp.float32
    )
    back_slots = bring_back(input_term, cols, group_size)
    picked = jnp.einsum("st,sd->td", placing, out_slots, preferred_element_type=jnp.float32)
    layer_out = (route_weight * picked).astype(jnp.bfloat16)
    token_grad = jnp.einsum(
        "st,sd->td", placing, back_slots, preferred_element_type=jnp.float32
    ).astype(jnp.bfloat16)
    gate_grad = jnp.einsum("nh,nd->hd", gate_grad_pre, token_rows, preferred_element_type=jnp.float32)
    up_grad = jnp.einsum("nh,nd->hd", up_grad_pre, token_rows, preferred_element_type=jnp.float32)
    down_grad = jnp.einsum("nh,nd->hd", hidden, grad_rows, preferred_element_type=jnp.float32)
    return (
        layer_out,
        token_grad,
        gate_grad.astype(jnp.bfloat16),
        up_grad.astype(jnp.bfloat16),
        down_grad.astype(jnp.bfloat16),
    )


def dot_nt(a, b):
    return lax.dot_general(a, b, (((1,), (1,)), ((), ())), preferred_element_type=jnp.float32)


def dot_tn(a, b):
    return lax.dot_general(a, b, (((0,), (0,)), ((), ())), preferred_element_type=jnp.float32)


def dot_nn(a, b):
    return jnp.dot(a, b, preferred_element_type=jnp.float32)


def fused_kernel(
    n_dp,
    ids_ref,
    weight_ref,
    row_key_ref,
    lane_key_ref,
    tokens_ref,
    cot_ref,
    w_gate_ref,
    w_up_ref,
    w_down_ref,
    final,
    big,
    gate_grad_ref,
    up_grad_ref,
    down_grad_ref,
    slots,
    pieces,
    raw,
    rows,
    partial,
    own_partial,
    summed_in,
    relayed,
    hidden_all,
    back_out,
    back_in,
    pick,
    spread_send,
    spread_recv,
    piece_send,
    piece_recv,
    sum_send,
    sum_recv,
    hid_send,
    hid_recv,
    ret_send,
    ret_recv,
    fin_send,
    fin_recv,
):
    n_ex = EXPERTS
    n_tok = tokens_ref.shape[0]
    cols = w_gate_ref.shape[1]
    width = w_gate_ref.shape[0]
    chunks = cols // LANES
    block = chunks * CAP
    group_rows = n_ex * CAP
    half = group_rows // 2
    d = lax.axis_index("dp")
    e = lax.axis_index("expert")

    across_x = d + 1 - 2 * lax.rem(d, 2)
    peers = (d, across_x, lax.rem(d + 2, 4), 3 - d)

    def dp_at(k):
        return peers[k]

    def ex_at(k):
        return lax.rem(e + k + n_ex, n_ex)

    def copy(src, dst, send_sem, recv_sem, to_dp, to_ex):
        return pltpu.make_async_remote_copy(
            src_ref=src,
            dst_ref=dst,
            send_sem=send_sem,
            recv_sem=recv_sem,
            device_id=(to_dp, to_ex),
            device_id_type=MESH,
        )

    barrier = pltpu.get_barrier_semaphore()
    for k in range(1, n_ex):
        pl.semaphore_signal(barrier, inc=1, device_id=(d, ex_at(k)), device_id_type=MESH)
    for k in range(1, n_dp):
        pl.semaphore_signal(barrier, inc=1, device_id=(dp_at(k), e), device_id_type=MESH)

    ids = ids_ref[...]
    onehot = ids == lax.broadcasted_iota(jnp.int32, (n_ex, n_tok), 0)
    onehot_f = onehot.astype(jnp.float32)
    earlier = (
        lax.broadcasted_iota(jnp.int32, (n_tok, n_tok), 0)
        < lax.broadcasted_iota(jnp.int32, (n_tok, n_tok), 1)
    ).astype(jnp.bfloat16)
    before = dot_nn(onehot_f.astype(jnp.bfloat16), earlier)
    place = jnp.sum(onehot_f * before, axis=0, keepdims=True).astype(jnp.int32)
    slot = ids * CAP + place
    row_key = row_key_ref[...]
    for c in range(chunks):
        big[:, c * n_tok : (c + 1) * n_tok] = (
            (row_key == slot + c * group_rows).astype(jnp.float32).astype(jnp.bfloat16)
        )
    lane_key = lane_key_ref[...]
    for c in range(chunks):
        want = lax.broadcasted_iota(jnp.int32, (group_rows, 1), 0) + c * group_rows
        pick[c] = (lane_key == want).astype(jnp.float32).astype(jnp.bfloat16)

    started = []

    def spread(a, source):
        for j in range(n_dp):
            stack = jnp.concatenate(
                [
                    source[:, j * cols + c * LANES : j * cols + (c + 1) * LANES]
                    for c in range(chunks)
                ],
                axis=0,
            )
            placed = dot_nn(big[...], stack).astype(jnp.bfloat16)
            slots[a, j] = placed.reshape(n_ex, block, LANES)

    def send_pieces(a):
        for kd in range(1, n_dp):
            to = dp_at(kd)
            cp = copy(
                slots.at[a, to],
                pieces.at[a, kd - 1],
                spread_send.at[a, kd],
                spread_recv.at[a, kd],
                to,
                e,
            )
            cp.start()
            started.append(cp)

    def forward(a, kd):
        if kd > 0:
            dst = pieces.at[a, kd - 1]
            copy(
                dst, dst, spread_send.at[a, kd], spread_recv.at[a, kd], dp_at(kd), e
            ).wait_recv()
            held = pieces.at[a, kd - 1]
        else:
            held = slots.at[a, d]
        for k in range(1, n_ex):
            to = ex_at(k)
            cp = copy(
                held.at[to],
                raw.at[a, kd, e],
                piece_send.at[a, kd, k],
                piece_recv.at[a, kd, k],
                d,
                to,
            )
            cp.start()
            started.append(cp)
        raw[a, kd, e] = held[e]

    spread(0, tokens_ref[...])
    pl.semaphore_wait(barrier, n_ex - 1 + n_dp - 1)
    send_pieces(0)
    forward(0, 0)
    spread(1, (weight_ref[...] * cot_ref[...].astype(jnp.float32)).astype(jnp.bfloat16))
    send_pieces(1)

    def arrange(a, kd):
        for k in range(1, n_ex):
            source = ex_at(-k)
            dst = raw.at[a, kd, source]
            copy(
                dst, dst, piece_send.at[a, kd, k], piece_recv.at[a, kd, k], d, source
            ).wait_recv()
        arrived = raw[a, kd].reshape(n_ex * block, LANES)
        for c in range(chunks):
            rows[a, kd, :, c * LANES : (c + 1) * LANES] = dot_nn(pick[c], arrived).astype(
                jnp.bfloat16
            )

    upper, lower = pl.ds(0, half), pl.ds(half, half)

    def send_sum(m, i, src, to):
        cp = copy(src, summed_in.at[m, i], sum_send.at[m, i], sum_recv.at[m, i], dp_at(to), e)
        cp.start()
        started.append(cp)

    def wait_sum(m, i, source):
        dst = summed_in.at[m, i]
        copy(dst, dst, sum_send.at[m, i], sum_recv.at[m, i], dp_at(source), e).wait_recv()

    def multiply(m, a, kd, w_ref):
        value = dot_nt(rows[a, kd], w_ref[...])
        if kd == 0:
            own_partial[m] = value
            return
        partial[m, kd - 1] = value.astype(jnp.bfloat16)
        if kd == 1:
            send_sum(m, 0, partial.at[m, 0, upper], 1)
        elif kd == 2:
            send_sum(m, 2, partial.at[m, 1, lower], 2)
        else:
            send_sum(m, 1, partial.at[m, 2, upper], 1)
            send_sum(m, 3, partial.at[m, 2, lower], 2)

    def relay_sum(m):
        wait_sum(m, 1, 1)
        relayed[m, 0] = (
            partial[m, 1, :half].astype(jnp.float32) + summed_in[m, 1].astype(jnp.float32)
        ).astype(jnp.bfloat16)
        send_sum(m, 4, relayed.at[m, 0], 2)
        wait_sum(m, 3, 2)
        relayed[m, 1] = (
            partial[m, 0, half:].astype(jnp.float32) + summed_in[m, 3].astype(jnp.float32)
        ).astype(jnp.bfloat16)
        send_sum(m, 5, relayed.at[m, 1], 1)

    def total(m):
        wait_sum(m, 0, 1)
        wait_sum(m, 2, 2)
        wait_sum(m, 4, 2)
        wait_sum(m, 5, 1)
        own = own_partial[m]
        top = own[:half] + (
            summed_in[m, 0].astype(jnp.float32) + summed_in[m, 4].astype(jnp.float32)
        )
        bottom = own[half:] + (
            summed_in[m, 2].astype(jnp.float32) + summed_in[m, 5].astype(jnp.float32)
        )
        return jnp.concatenate([top, bottom], axis=0)

    forward(0, 1)
    forward(0, 2)
    forward(0, 3)
    forward(1, 0)
    for kd in range(n_dp):
        arrange(0, kd)
        multiply(0, 0, kd, w_gate_ref)
        multiply(1, 0, kd, w_up_ref)
        if kd == 0:
            for other in range(1, n_dp):
                forward(1, other)
    relay_sum(0)
    relay_sum(1)
    for kd in range(n_dp):
        arrange(1, kd)
        multiply(2, 1, kd, w_down_ref)

    def send_hidden(m, kd, src, dst, to):
        cp = copy(src, dst, hid_send.at[m, kd], hid_recv.at[m, kd], dp_at(to), e)
        cp.start()
        started.append(cp)

    def await_hidden(m, kd, dst, source):
        copy(dst, dst, hid_send.at[m, kd], hid_recv.at[m, kd], dp_at(source), e).wait_recv()

    def share(m, value):
        hidden_all[m, 0] = value
        for kd in (1, 2):
            send_hidden(m, kd, hidden_all.at[m, 0], hidden_all.at[m, kd], kd)

    def relay_hidden(m):
        await_hidden(m, 1, hidden_all.at[m, 1], 1)
        send_hidden(m, 3, hidden_all.at[m, 1, lower], hidden_all.at[m, 3, lower], 2)
        await_hidden(m, 2, hidden_all.at[m, 2], 2)
        send_hidden(m, 0, hidden_all.at[m, 2, upper], hidden_all.at[m, 3, upper], 1)

    def last_hidden(m):
        await_hidden(m, 3, hidden_all.at[m, 3, lower], 2)
        await_hidden(m, 0, hidden_all.at[m, 3, upper], 1)

    gate_pre = total(0)
    sigmoid = 1.0 / (1.0 + jnp.exp(-gate_pre))
    silu = gate_pre * sigmoid
    own_partial[0] = silu
    up_pre = total(1)
    share(0, (silu * up_pre).astype(jnp.bfloat16))
    own_partial[1] = up_pre * (sigmoid * (1.0 + gate_pre * (1.0 - sigmoid)))
    relay_sum(2)
    hidden_grad = total(2)
    share(1, (hidden_grad * own_partial[1]).astype(jnp.bfloat16))
    share(2, (hidden_grad * own_partial[0]).astype(jnp.bfloat16))

    def send_back(b, kd, value):
        value = value.astype(jnp.bfloat16)
        back = dot_tn(pick[0], value[:, :LANES])
        for c in range(1, chunks):
            back = back + dot_tn(pick[c], value[:, c * LANES : (c + 1) * LANES])
        back = back.astype(jnp.bfloat16).reshape(n_ex, block, LANES)
        if kd == 0:
            back_in[b, 0] = back
            return
        back_out[b, kd - 1] = back
        cp = copy(
            back_out.at[b, kd - 1],
            back_in.at[b, kd],
            ret_send.at[b, kd],
            ret_recv.at[b, kd],
            dp_at(kd),
            e,
        )
        cp.start()
        started.append(cp)

    def finish_send(b, kd):
        if kd > 0:
            copy(
                back_in.at[b, kd],
                back_in.at[b, kd],
                ret_send.at[b, kd],
                ret_recv.at[b, kd],
                dp_at(kd),
                e,
            ).wait_recv()
        j = dp_at(kd)
        for k in range(1, n_ex):
            to = ex_at(k)
            cp = copy(
                back_in.at[b, kd, to],
                final.at[b, j, e],
                fin_send.at[b, kd, k],
                fin_recv.at[b, kd, k],
                d,
                to,
            )
            cp.start()
            started.append(cp)
        final[b, j, e] = back_in[b, kd, e]

    def output(kd):
        send_back(0, kd, dot_nn(hidden_all[0, kd], w_down_ref[...]))

    def input_grad(kd):
        send_back(
            1,
            kd,
            dot_nn(hidden_all[1, kd], w_gate_ref[...]) + dot_nn(hidden_all[2, kd], w_up_ref[...]),
        )

    tile = 256 if width % 256 == 0 else width

    def weight_grad(m, a, out_ref):
        right = rows[a].reshape(n_dp * group_rows, cols)
        for t in range(width // tile):
            left = hidden_all[m, :, :, t * tile : (t + 1) * tile].reshape(n_dp * group_rows, tile)
            out_ref[t * tile : (t + 1) * tile, :] = dot_tn(left, right).astype(jnp.bfloat16)

    relay_hidden(0)
    for kd in (1, 2, 0):
        output(kd)
    finish_send(0, 0)
    relay_hidden(1)
    relay_hidden(2)
    last_hidden(0)
    output(3)
    finish_send(0, 1)
    finish_send(0, 2)
    for kd in (1, 2, 0):
        input_grad(kd)
    finish_send(1, 0)
    finish_send(0, 3)
    weight_grad(0, 1, down_grad_ref)
    last_hidden(1)
    last_hidden(2)
    input_grad(3)
    finish_send(1, 1)
    finish_send(1, 2)
    weight_grad(1, 0, gate_grad_ref)
    finish_send(1, 3)
    weight_grad(2, 0, up_grad_ref)

    for b in range(2):
        for kd in range(n_dp):
            for k in range(1, n_ex):
                source = ex_at(-k)
                copy(
                    final.at[b, dp_at(kd), source],
                    final.at[b, dp_at(kd), source],
                    fin_send.at[b, kd, k],
                    fin_recv.at[b, kd, k],
                    d,
                    source,
                ).wait_recv()
    for cp in started:
        cp.wait_send()


def finish_kernel(
    weight_ref,
    big_ref,
    final_ref,
    gate_in,
    up_in,
    down_in,
    layer_out_ref,
    token_grad_ref,
    gate_out,
    up_out,
    down_out,
    held,
    in_sems,
    out_sems,
):
    loads = [
        pltpu.make_async_copy(src, held.at[i], in_sems.at[i])
        for i, src in enumerate((gate_in, up_in, down_in))
    ]
    stores = [
        pltpu.make_async_copy(held.at[i], dst, out_sems.at[i])
        for i, dst in enumerate((gate_out, up_out, down_out))
    ]
    for cp in loads:
        cp.start()
    n_tok = weight_ref.shape[0]
    n_dp = final_ref.shape[1]
    chunks = big_ref.shape[1] // n_tok
    cols = chunks * LANES
    for b, out_ref in ((0, layer_out_ref), (1, token_grad_ref)):
        for j in range(n_dp):
            value = dot_tn(big_ref[...], final_ref[b, j].reshape(big_ref.shape[0], LANES))
            for c in range(chunks):
                piece = value[c * n_tok : (c + 1) * n_tok]
                if b == 0:
                    piece = weight_ref[...] * piece
                out_ref[:, j * cols + c * LANES : j * cols + (c + 1) * LANES] = piece.astype(
                    jnp.bfloat16
                )
            if b == 0 and j < len(loads):
                loads[j].wait()
                stores[j].start()
    for cp in stores:
        cp.wait()


def local_fused(tokens, expert_ids, route_weight, cotangent, w_gate, w_up, w_down):
    n_dp = lax.axis_size("dp")
    n_ex = lax.axis_size("expert")
    n_tok, features = tokens.shape
    width, cols = w_gate.shape
    chunks = cols // LANES
    block = chunks * CAP
    group_rows = n_ex * CAP
    at = np.arange(n_ex * block)
    key = (at // block) * CAP + at % CAP + ((at % block) // CAP) * group_rows
    key = key.astype(np.int32)
    bf16 = jnp.bfloat16
    vmem = pl.BlockSpec(memory_space=pltpu.VMEM)
    dma = pltpu.SemaphoreType.DMA
    vmem_limit = 56 * 1024 * 1024
    weight_struct = jax.ShapeDtypeStruct((width, cols), bf16)
    token_struct = jax.ShapeDtypeStruct((n_tok, features), bf16)
    final, big, gate_grad, up_grad, down_grad = pl.pallas_call(
        functools.partial(fused_kernel, n_dp),
        out_shape=(
            jax.ShapeDtypeStruct((2, n_dp, n_ex, block, LANES), bf16),
            jax.ShapeDtypeStruct((n_ex * block, chunks * n_tok), bf16),
            weight_struct,
            weight_struct,
            weight_struct,
        ),
        in_specs=[vmem] * 9,
        out_specs=(vmem,) * 5,
        scratch_shapes=[
            pltpu.VMEM((2, n_dp, n_ex, block, LANES), bf16),
            pltpu.VMEM((2, n_dp - 1, n_ex, block, LANES), bf16),
            pltpu.VMEM((2, n_dp, n_ex, block, LANES), bf16),
            pltpu.VMEM((2, n_dp, group_rows, cols), bf16),
            pltpu.VMEM((3, n_dp - 1, group_rows, width), bf16),
            pltpu.VMEM((3, group_rows, width), jnp.float32),
            pltpu.VMEM((3, 6, group_rows // 2, width), bf16),
            pltpu.VMEM((3, 2, group_rows // 2, width), bf16),
            pltpu.VMEM((3, n_dp, group_rows, width), bf16),
            pltpu.VMEM((2, n_dp - 1, n_ex, block, LANES), bf16),
            pltpu.VMEM((2, n_dp, n_ex, block, LANES), bf16),
            pltpu.VMEM((chunks, group_rows, n_ex * block), bf16),
            dma((2, n_dp)),
            dma((2, n_dp)),
            dma((2, n_dp, n_ex)),
            dma((2, n_dp, n_ex)),
            dma((3, 6)),
            dma((3, 6)),
            dma((3, n_dp)),
            dma((3, n_dp)),
            dma((2, n_dp)),
            dma((2, n_dp)),
            dma((2, n_dp, n_ex)),
            dma((2, n_dp, n_ex)),
        ],
        compiler_params=pltpu.CompilerParams(
            collective_id=0, has_side_effects=True, vmem_limit_bytes=vmem_limit
        ),
        cost_estimate=pl.CostEstimate(
            flops=18 * n_dp * group_rows * width * cols,
            bytes_accessed=12 * width * cols + 8 * n_tok * features,
            transcendentals=group_rows * width,
        ),
    )(
        expert_ids.reshape(1, n_tok),
        route_weight,
        jnp.asarray(key)[:, None],
        jnp.asarray(key)[None, :],
        tokens,
        cotangent,
        w_gate,
        w_up,
        w_down,
    )
    hbm = pl.BlockSpec(memory_space=pl.ANY)
    return pl.pallas_call(
        finish_kernel,
        out_shape=(token_struct, token_struct, weight_struct, weight_struct, weight_struct),
        in_specs=[vmem] * 3 + [hbm] * 3,
        out_specs=(vmem,) * 2 + (hbm,) * 3,
        scratch_shapes=[pltpu.VMEM((3, width, cols), bf16), dma((3,)), dma((3,))],
        compiler_params=pltpu.CompilerParams(vmem_limit_bytes=vmem_limit),
    )(route_weight, big, final, gate_grad, up_grad, down_grad)


def solution(mesh):
    one_block = mesh.shape["expert"] == EXPERTS and mesh.shape["dp"] == 4
    return jax.shard_map(
        local_fused if one_block else local,
        mesh=mesh,
        in_specs=(
            P(BOTH, None),
            P(BOTH, None),
            P(BOTH, None),
            P(BOTH, None),
            P("expert", "dp"),
            P("expert", "dp"),
            P("expert", "dp"),
        ),
        out_specs=(
            P(BOTH, None),
            P(BOTH, None),
            P("expert", "dp"),
            P("expert", "dp"),
            P("expert", "dp"),
        ),
        check_vma=False,
    )
```

```python
import functools

import jax
import jax.numpy as jnp
import numpy as np
from jax import lax
from jax.experimental import pallas as pl
from jax.experimental.pallas import tpu as pltpu
from jax.sharding import PartitionSpec as P

EXPERTS = 8
CAP = 20
BOTH = ("dp", "expert")
LANES = 128
MESH = pl.DeviceIdType.MESH


def spread(slots, cols, group_size):
    n_dp = lax.axis_size("dp")
    pieces = slots.reshape(EXPERTS, CAP, n_dp, cols).transpose(2, 0, 1, 3)
    sending = jnp.repeat(pieces, group_size, axis=1).reshape(-1, CAP, cols)
    arrived = lax.all_to_all(sending, BOTH, split_axis=0, concat_axis=0, tiled=True)
    return arrived.reshape(-1, cols)


def bring_back(rows, cols, group_size):
    n_dp = lax.axis_size("dp")
    sending = rows.astype(jnp.bfloat16).reshape(-1, CAP, cols)
    arrived = lax.all_to_all(sending, BOTH, split_axis=0, concat_axis=0, tiled=True)
    pieces = arrived.reshape(n_dp, EXPERTS, group_size, CAP, cols)
    if group_size > 1:
        pieces = jnp.sum(pieces.astype(jnp.float32), axis=2).astype(jnp.bfloat16)
    else:
        pieces = pieces[:, :, 0]
    return pieces.transpose(1, 2, 0, 3).reshape(EXPERTS * CAP, n_dp * cols)


def scatter_sum(partial):
    return lax.psum_scatter(
        partial.astype(jnp.bfloat16), "dp", scatter_dimension=0, tiled=True
    ).astype(jnp.float32)


def local(tokens, expert_ids, route_weight, cotangent, w_gate, w_up, w_down):
    cols = w_gate.shape[1]
    group_size = lax.axis_size("expert") // EXPERTS
    chosen = expert_ids[:, 0]
    onehot = (chosen[:, None] == jnp.arange(EXPERTS, dtype=jnp.int32)[None, :]).astype(jnp.int32)
    before = jnp.cumsum(onehot, axis=0) - onehot
    slot_index = chosen * CAP + jnp.sum(before * onehot, axis=1)
    placing = (jnp.arange(EXPERTS * CAP, dtype=jnp.int32)[:, None] == slot_index[None, :]).astype(
        jnp.bfloat16
    )
    scaled = (route_weight * cotangent.astype(jnp.float32)).astype(jnp.bfloat16)
    token_slots = jnp.dot(placing, tokens, preferred_element_type=jnp.float32).astype(jnp.bfloat16)
    grad_slots = jnp.dot(placing, scaled, preferred_element_type=jnp.float32).astype(jnp.bfloat16)
    token_rows = spread(token_slots, cols, group_size)
    gate_pre = scatter_sum(
        jnp.einsum("nd,hd->nh", token_rows, w_gate, preferred_element_type=jnp.float32)
    )
    up_pre = scatter_sum(
        jnp.einsum("nd,hd->nh", token_rows, w_up, preferred_element_type=jnp.float32)
    )
    grad_rows = spread(grad_slots, cols, group_size)
    hidden_grad = scatter_sum(
        jnp.einsum("nd,hd->nh", grad_rows, w_down, preferred_element_type=jnp.float32)
    )
    gate_sigmoid = jax.nn.sigmoid(gate_pre)
    gate_silu = gate_pre * gate_sigmoid
    hidden = (gate_silu * up_pre).astype(jnp.bfloat16)
    hidden = lax.all_gather(hidden, "dp", axis=0, tiled=True)
    gate_grad_pre = (
        hidden_grad * up_pre * (gate_sigmoid * (1.0 + gate_pre * (1.0 - gate_sigmoid)))
    ).astype(jnp.bfloat16)
    gate_grad_pre = lax.all_gather(gate_grad_pre, "dp", axis=0, tiled=True)
    up_grad_pre = (hidden_grad * gate_silu).astype(jnp.bfloat16)
    up_grad_pre = lax.all_gather(up_grad_pre, "dp", axis=0, tiled=True)
    out_slots = bring_back(
        jnp.dot(hidden, w_down, preferred_element_type=jnp.float32), cols, group_size
    )
    input_term = jnp.dot(gate_grad_pre, w_gate, preferred_element_type=jnp.float32) + jnp.dot(
        up_grad_pre, w_up, preferred_element_type=jnp.float32
    )
    back_slots = bring_back(input_term, cols, group_size)
    picked = jnp.einsum("st,sd->td", placing, out_slots, preferred_element_type=jnp.float32)
    layer_out = (route_weight * picked).astype(jnp.bfloat16)
    token_grad = jnp.einsum(
        "st,sd->td", placing, back_slots, preferred_element_type=jnp.float32
    ).astype(jnp.bfloat16)
    gate_grad = jnp.einsum("nh,nd->hd", gate_grad_pre, token_rows, preferred_element_type=jnp.float32)
    up_grad = jnp.einsum("nh,nd->hd", up_grad_pre, token_rows, preferred_element_type=jnp.float32)
    down_grad = jnp.einsum("nh,nd->hd", hidden, grad_rows, preferred_element_type=jnp.float32)
    return (
        layer_out,
        token_grad,
        gate_grad.astype(jnp.bfloat16),
        up_grad.astype(jnp.bfloat16),
        down_grad.astype(jnp.bfloat16),
    )


def dot_nt(a, b):
    return lax.dot_general(a, b, (((1,), (1,)), ((), ())), preferred_element_type=jnp.float32)


def dot_tn(a, b):
    return lax.dot_general(a, b, (((0,), (0,)), ((), ())), preferred_element_type=jnp.float32)


def dot_nn(a, b):
    return jnp.dot(a, b, preferred_element_type=jnp.float32)


def weight_column(row):
    n = row.shape[1]
    same = lax.broadcasted_iota(jnp.int32, (n, n), 0) == lax.broadcasted_iota(jnp.int32, (n, n), 1)
    return jnp.sum(jnp.where(same, row, 0.0), axis=1, keepdims=True)


def fused_kernel(
    n_dp,
    ids_ref,
    weight_ref,
    row_key_ref,
    lane_key_ref,
    tokens_ref,
    cot_ref,
    w_gate_in,
    w_up_in,
    w_down_in,
    final,
    big_t,
    gate_grad_out,
    up_grad_out,
    down_grad_out,
    big,
    w_gate_ref,
    w_up_ref,
    w_down_ref,
    gate_grad_ref,
    up_grad_ref,
    down_grad_ref,
    slots,
    pieces,
    raw,
    rows,
    partial,
    own_partial,
    summed_in,
    relayed,
    hidden_all,
    back_out,
    back_in,
    gather,
    ungather,
    spread_send,
    spread_recv,
    piece_send,
    piece_recv,
    sum_send,
    sum_recv,
    hid_send,
    hid_recv,
    ret_send,
    ret_recv,
    fin_send,
    fin_recv,
    load_sem,
    store_sem,
):
    loads = [
        pltpu.make_async_copy(src, dst, load_sem.at[i])
        for i, (src, dst) in enumerate(
            ((w_gate_in, w_gate_ref), (w_up_in, w_up_ref), (w_down_in, w_down_ref))
        )
    ]
    for cp in loads:
        cp.start()
    n_ex = EXPERTS
    n_tok = tokens_ref.shape[0]
    cols = w_gate_in.shape[1]
    width = w_gate_in.shape[0]
    chunks = cols // LANES
    block = chunks * CAP
    group_rows = n_ex * CAP
    half = group_rows // 2
    d = lax.axis_index("dp")
    e = lax.axis_index("expert")

    across_x = d + 1 - 2 * lax.rem(d, 2)
    peers = (d, across_x, lax.rem(d + 2, 4), 3 - d)

    def dp_at(k):
        return peers[k]

    def ex_at(k):
        return lax.rem(e + k + n_ex, n_ex)

    def copy(src, dst, send_sem, recv_sem, to_dp, to_ex):
        return pltpu.make_async_remote_copy(
            src_ref=src,
            dst_ref=dst,
            send_sem=send_sem,
            recv_sem=recv_sem,
            device_id=(to_dp, to_ex),
            device_id_type=MESH,
        )

    barrier = pltpu.get_barrier_semaphore()
    for k in range(1, n_ex):
        pl.semaphore_signal(barrier, inc=1, device_id=(d, ex_at(k)), device_id_type=MESH)
    for k in range(1, n_dp):
        pl.semaphore_signal(barrier, inc=1, device_id=(dp_at(k), e), device_id_type=MESH)

    ids = ids_ref[...]
    onehot = ids == lax.broadcasted_iota(jnp.int32, (n_ex, n_tok), 0)
    onehot_f = onehot.astype(jnp.float32)
    earlier = (
        lax.broadcasted_iota(jnp.int32, (n_tok, n_tok), 0)
        < lax.broadcasted_iota(jnp.int32, (n_tok, n_tok), 1)
    ).astype(jnp.bfloat16)
    before = dot_nn(onehot_f.astype(jnp.bfloat16), earlier)
    place = jnp.sum(onehot_f * before, axis=0, keepdims=True).astype(jnp.int32)
    slot = ids * CAP + place
    row_key = row_key_ref[...]
    for c in range(chunks):
        big[:, c * n_tok : (c + 1) * n_tok] = (
            (row_key == slot + c * group_rows).astype(jnp.float32).astype(jnp.bfloat16)
        )
    started = []

    def spread(a, source):
        stack = jnp.concatenate(
            [
                jnp.concatenate(
                    [
                        source[:, j * cols + c * LANES : j * cols + (c + 1) * LANES]
                        for j in range(n_dp)
                    ],
                    axis=1,
                )
                for c in range(chunks)
            ],
            axis=0,
        )
        placed = dot_nn(big[...], stack).astype(jnp.bfloat16)
        for j in range(n_dp):
            slots[a, j] = placed[:, j * LANES : (j + 1) * LANES].reshape(n_ex, block, LANES)

    def send_pieces(a):
        for kd in range(1, n_dp):
            to = dp_at(kd)
            cp = copy(
                slots.at[a, to],
                pieces.at[a, kd - 1],
                spread_send.at[a, kd],
                spread_recv.at[a, kd],
                to,
                e,
            )
            cp.start()
            started.append(cp)

    def forward(a, kd):
        if kd > 0:
            dst = pieces.at[a, kd - 1]
            copy(
                dst, dst, spread_send.at[a, kd], spread_recv.at[a, kd], dp_at(kd), e
            ).wait_recv()
            held = pieces.at[a, kd - 1]
        else:
            held = slots.at[a, d]
        for k in range(1, n_ex):
            to = ex_at(k)
            cp = copy(
                held.at[to],
                raw.at[a, kd, e],
                piece_send.at[a, kd, k],
                piece_recv.at[a, kd, k],
                d,
                to,
            )
            cp.start()
            started.append(cp)
        raw[a, kd, e] = held[e]

    spread(0, tokens_ref[...])
    pl.semaphore_wait(barrier, n_ex - 1 + n_dp - 1)
    send_pieces(0)
    forward(0, 0)
    weight = weight_column(weight_ref[...])
    spread(1, (weight * cot_ref[...].astype(jnp.float32)).astype(jnp.bfloat16))
    send_pieces(1)
    lane_key = lane_key_ref[...]
    total_rows = n_ex * block
    want = lax.broadcasted_iota(jnp.int32, (total_rows, 1), 0)
    gather[...] = (lane_key == want).astype(jnp.float32).astype(jnp.bfloat16)
    want = lax.broadcasted_iota(jnp.int32, (1, total_rows), 1)
    ungather[...] = (row_key == want).astype(jnp.float32).astype(jnp.bfloat16)

    big_t[...] = big[...].T
    for cp in loads:
        cp.wait()

    def arrange(a, kd):
        for k in range(1, n_ex):
            source = ex_at(-k)
            dst = raw.at[a, kd, source]
            copy(
                dst, dst, piece_send.at[a, kd, k], piece_recv.at[a, kd, k], d, source
            ).wait_recv()
        arrived = raw[a, kd].reshape(n_ex * block, LANES)
        ordered = dot_nn(gather[...], arrived).astype(jnp.bfloat16)
        for c in range(chunks):
            rows[a, kd, :, c * LANES : (c + 1) * LANES] = ordered[
                c * group_rows : (c + 1) * group_rows
            ]

    upper, lower = pl.ds(0, half), pl.ds(half, half)

    def send_sum(m, i, src, to):
        cp = copy(src, summed_in.at[m, i], sum_send.at[m, i], sum_recv.at[m, i], dp_at(to), e)
        cp.start()
        started.append(cp)

    def wait_sum(m, i, source):
        dst = summed_in.at[m, i]
        copy(dst, dst, sum_send.at[m, i], sum_recv.at[m, i], dp_at(source), e).wait_recv()

    def multiply(m, a, kd, w_ref):
        value = dot_nt(rows[a, kd], w_ref[...])
        if kd == 0:
            own_partial[m] = value
            return
        partial[m, kd - 1] = value.astype(jnp.bfloat16)
        if kd == 1:
            send_sum(m, 0, partial.at[m, 0, upper], 1)
        elif kd == 2:
            send_sum(m, 2, partial.at[m, 1, lower], 2)
        else:
            send_sum(m, 1, partial.at[m, 2, upper], 1)
            send_sum(m, 3, partial.at[m, 2, lower], 2)

    def relay_sum(m):
        wait_sum(m, 1, 1)
        relayed[m, 0] = (
            partial[m, 1, :half].astype(jnp.float32) + summed_in[m, 1].astype(jnp.float32)
        ).astype(jnp.bfloat16)
        send_sum(m, 4, relayed.at[m, 0], 2)
        wait_sum(m, 3, 2)
        relayed[m, 1] = (
            partial[m, 0, half:].astype(jnp.float32) + summed_in[m, 3].astype(jnp.float32)
        ).astype(jnp.bfloat16)
        send_sum(m, 5, relayed.at[m, 1], 1)

    def total(m):
        wait_sum(m, 0, 1)
        wait_sum(m, 2, 2)
        wait_sum(m, 4, 2)
        wait_sum(m, 5, 1)
        own = own_partial[m]
        top = own[:half] + (
            summed_in[m, 0].astype(jnp.float32) + summed_in[m, 4].astype(jnp.float32)
        )
        bottom = own[half:] + (
            summed_in[m, 2].astype(jnp.float32) + summed_in[m, 5].astype(jnp.float32)
        )
        return jnp.concatenate([top, bottom], axis=0)

    forward(0, 1)
    forward(0, 2)
    forward(0, 3)
    forward(1, 0)
    for kd in range(n_dp):
        arrange(0, kd)
        multiply(0, 0, kd, w_gate_ref)
        multiply(1, 0, kd, w_up_ref)
        if kd == 0:
            for other in range(1, n_dp):
                forward(1, other)
    relay_sum(0)
    relay_sum(1)
    for kd in range(n_dp):
        arrange(1, kd)
        multiply(2, 1, kd, w_down_ref)

    def send_hidden(m, kd, src, dst, to):
        cp = copy(src, dst, hid_send.at[m, kd], hid_recv.at[m, kd], dp_at(to), e)
        cp.start()
        started.append(cp)

    def await_hidden(m, kd, dst, source):
        copy(dst, dst, hid_send.at[m, kd], hid_recv.at[m, kd], dp_at(source), e).wait_recv()

    def share(m, value):
        hidden_all[m, 0] = value
        for kd in (1, 2):
            send_hidden(m, kd, hidden_all.at[m, 0], hidden_all.at[m, kd], kd)

    def relay_hidden(m):
        await_hidden(m, 1, hidden_all.at[m, 1], 1)
        send_hidden(m, 3, hidden_all.at[m, 1, lower], hidden_all.at[m, 3, lower], 2)
        await_hidden(m, 2, hidden_all.at[m, 2], 2)
        send_hidden(m, 0, hidden_all.at[m, 2, upper], hidden_all.at[m, 3, upper], 1)

    def last_hidden(m):
        await_hidden(m, 3, hidden_all.at[m, 3, lower], 2)
        await_hidden(m, 0, hidden_all.at[m, 3, upper], 1)

    gate_pre = total(0)
    sigmoid = 1.0 / (1.0 + jnp.exp(-gate_pre))
    silu = gate_pre * sigmoid
    own_partial[0] = silu
    up_pre = total(1)
    share(0, (silu * up_pre).astype(jnp.bfloat16))
    own_partial[1] = up_pre * (sigmoid * (1.0 + gate_pre * (1.0 - sigmoid)))
    relay_sum(2)
    hidden_grad = total(2)
    share(1, (hidden_grad * own_partial[1]).astype(jnp.bfloat16))
    share(2, (hidden_grad * own_partial[0]).astype(jnp.bfloat16))

    def send_back(b, kd, value):
        value = value.astype(jnp.bfloat16)
        stack = jnp.concatenate(
            [value[:, c * LANES : (c + 1) * LANES] for c in range(chunks)], axis=0
        )
        back = dot_nn(ungather[...], stack).astype(jnp.bfloat16).reshape(n_ex, block, LANES)
        if kd == 0:
            back_in[b, 0] = back
            return
        back_out[b, kd - 1] = back
        cp = copy(
            back_out.at[b, kd - 1],
            back_in.at[b, kd],
            ret_send.at[b, kd],
            ret_recv.at[b, kd],
            dp_at(kd),
            e,
        )
        cp.start()
        started.append(cp)

    def finish_send(b, kd):
        if kd > 0:
            copy(
                back_in.at[b, kd],
                back_in.at[b, kd],
                ret_send.at[b, kd],
                ret_recv.at[b, kd],
                dp_at(kd),
                e,
            ).wait_recv()
        j = dp_at(kd)
        for k in range(1, n_ex):
            to = ex_at(k)
            cp = copy(
                back_in.at[b, kd, to],
                final.at[b, j, e],
                fin_send.at[b, kd, k],
                fin_recv.at[b, kd, k],
                d,
                to,
            )
            cp.start()
            started.append(cp)
        final[b, j, e] = back_in[b, kd, e]

    def output(kd):
        send_back(0, kd, dot_nn(hidden_all[0, kd], w_down_ref[...]))

    def input_grad(kd):
        send_back(
            1,
            kd,
            dot_nn(hidden_all[1, kd], w_gate_ref[...]) + dot_nn(hidden_all[2, kd], w_up_ref[...]),
        )

    tile = 256 if width % 256 == 0 else width

    stores = []

    def weight_grad(m, a, out_ref, hbm_ref):
        right = rows[a].reshape(n_dp * group_rows, cols)
        for t in range(width // tile):
            left = hidden_all[m, :, :, t * tile : (t + 1) * tile].reshape(n_dp * group_rows, tile)
            out_ref[t * tile : (t + 1) * tile, :] = dot_tn(left, right).astype(jnp.bfloat16)
        cp = pltpu.make_async_copy(out_ref, hbm_ref, store_sem.at[m])
        cp.start()
        stores.append(cp)

    relay_hidden(0)
    for kd in (1, 2, 0):
        output(kd)
    finish_send(0, 0)
    relay_hidden(1)
    relay_hidden(2)
    last_hidden(0)
    output(3)
    finish_send(0, 1)
    finish_send(0, 2)
    for kd in (1, 2, 0):
        input_grad(kd)
    finish_send(1, 0)
    finish_send(0, 3)
    last_hidden(1)
    last_hidden(2)
    input_grad(3)
    finish_send(1, 1)
    finish_send(1, 2)
    weight_grad(0, 1, down_grad_ref, down_grad_out)
    finish_send(1, 3)
    weight_grad(1, 0, gate_grad_ref, gate_grad_out)
    weight_grad(2, 0, up_grad_ref, up_grad_out)

    for b in range(2):
        for kd in range(n_dp):
            for k in range(1, n_ex):
                source = ex_at(-k)
                copy(
                    final.at[b, dp_at(kd), source],
                    final.at[b, dp_at(kd), source],
                    fin_send.at[b, kd, k],
                    fin_recv.at[b, kd, k],
                    d,
                    source,
                ).wait_recv()
    for cp in started:
        cp.wait_send()
    for cp in stores:
        cp.wait()


def finish_kernel(
    weight_ref,
    big_ref,
    final_ref,
    gate_in,
    up_in,
    down_in,
    layer_out_ref,
    token_grad_ref,
    gate_out,
    up_out,
    down_out,
    held,
    in_sems,
    out_sems,
):
    loads = [
        pltpu.make_async_copy(src, held.at[i], in_sems.at[i])
        for i, src in enumerate((gate_in, up_in, down_in))
    ]
    stores = [
        pltpu.make_async_copy(held.at[i], dst, out_sems.at[i])
        for i, dst in enumerate((gate_out, up_out, down_out))
    ]
    for cp in loads:
        cp.start()
    n_tok = weight_ref.shape[1]
    n_dp = final_ref.shape[1]
    chunks = big_ref.shape[0] // n_tok
    cols = chunks * LANES
    weight = weight_column(weight_ref[...])
    for b, out_ref in ((0, layer_out_ref), (1, token_grad_ref)):
        slots = jnp.concatenate(
            [final_ref[b, j].reshape(big_ref.shape[1], LANES) for j in range(n_dp)], axis=1
        )
        value = dot_nn(big_ref[...], slots)
        for c in range(chunks):
            piece = value[c * n_tok : (c + 1) * n_tok]
            if b == 0:
                piece = weight * piece
            piece = piece.astype(jnp.bfloat16)
            for j in range(n_dp):
                out_ref[:, j * cols + c * LANES : j * cols + (c + 1) * LANES] = piece[
                    :, j * LANES : (j + 1) * LANES
                ]
        if b == 0:
            for load, store in zip(loads, stores):
                load.wait()
                store.start()
    for cp in stores:
        cp.wait()


def local_fused(tokens, expert_ids, route_weight, cotangent, w_gate, w_up, w_down):
    n_dp = lax.axis_size("dp")
    n_ex = lax.axis_size("expert")
    n_tok, features = tokens.shape
    width, cols = w_gate.shape
    chunks = cols // LANES
    block = chunks * CAP
    group_rows = n_ex * CAP
    at = np.arange(n_ex * block)
    key = (at // block) * CAP + at % CAP + ((at % block) // CAP) * group_rows
    key = key.astype(np.int32)
    bf16 = jnp.bfloat16
    vmem = pl.BlockSpec(memory_space=pltpu.VMEM)
    hbm = pl.BlockSpec(memory_space=pl.ANY)
    dma = pltpu.SemaphoreType.DMA
    weight_row = route_weight.reshape(1, n_tok)
    vmem_limit = 56 * 1024 * 1024
    weight_struct = jax.ShapeDtypeStruct((width, cols), bf16)
    token_struct = jax.ShapeDtypeStruct((n_tok, features), bf16)
    final, big_t, gate_grad, up_grad, down_grad = pl.pallas_call(
        functools.partial(fused_kernel, n_dp),
        out_shape=(
            jax.ShapeDtypeStruct((2, n_dp, n_ex, block, LANES), bf16),
            jax.ShapeDtypeStruct((chunks * n_tok, n_ex * block), bf16),
            weight_struct,
            weight_struct,
            weight_struct,
        ),
        in_specs=[vmem] * 6 + [hbm] * 3,
        out_specs=(vmem,) * 2 + (hbm,) * 3,
        scratch_shapes=[
            pltpu.VMEM((n_ex * block, chunks * n_tok), bf16),
            *[pltpu.VMEM((width, cols), bf16) for _ in range(6)],
            pltpu.VMEM((2, n_dp, n_ex, block, LANES), bf16),
            pltpu.VMEM((2, n_dp - 1, n_ex, block, LANES), bf16),
            pltpu.VMEM((2, n_dp, n_ex, block, LANES), bf16),
            pltpu.VMEM((2, n_dp, group_rows, cols), bf16),
            pltpu.VMEM((3, n_dp - 1, group_rows, width), bf16),
            pltpu.VMEM((3, group_rows, width), jnp.float32),
            pltpu.VMEM((3, 6, group_rows // 2, width), bf16),
            pltpu.VMEM((3, 2, group_rows // 2, width), bf16),
            pltpu.VMEM((3, n_dp, group_rows, width), bf16),
            pltpu.VMEM((2, n_dp - 1, n_ex, block, LANES), bf16),
            pltpu.VMEM((2, n_dp, n_ex, block, LANES), bf16),
            pltpu.VMEM((n_ex * block, n_ex * block), bf16),
            pltpu.VMEM((n_ex * block, n_ex * block), bf16),
            dma((2, n_dp)),
            dma((2, n_dp)),
            dma((2, n_dp, n_ex)),
            dma((2, n_dp, n_ex)),
            dma((3, 6)),
            dma((3, 6)),
            dma((3, n_dp)),
            dma((3, n_dp)),
            dma((2, n_dp)),
            dma((2, n_dp)),
            dma((2, n_dp, n_ex)),
            dma((2, n_dp, n_ex)),
            dma((3,)),
            dma((3,)),
        ],
        compiler_params=pltpu.CompilerParams(
            collective_id=0, has_side_effects=True, vmem_limit_bytes=vmem_limit
        ),
        cost_estimate=pl.CostEstimate(
            flops=18 * n_dp * group_rows * width * cols,
            bytes_accessed=12 * width * cols + 8 * n_tok * features,
            transcendentals=group_rows * width,
        ),
    )(
        expert_ids.reshape(1, n_tok),
        weight_row,
        jnp.asarray(key)[:, None],
        jnp.asarray(key)[None, :],
        tokens,
        cotangent,
        w_gate,
        w_up,
        w_down,
    )
    return pl.pallas_call(
        finish_kernel,
        out_shape=(token_struct, token_struct, weight_struct, weight_struct, weight_struct),
        in_specs=[vmem] * 3 + [hbm] * 3,
        out_specs=(vmem,) * 2 + (hbm,) * 3,
        scratch_shapes=[pltpu.VMEM((3, width, cols), bf16), dma((3,)), dma((3,))],
        compiler_params=pltpu.CompilerParams(vmem_limit_bytes=vmem_limit),
    )(weight_row, big_t, final, gate_grad, up_grad, down_grad)


def solution(mesh):
    one_block = mesh.shape["expert"] == EXPERTS and mesh.shape["dp"] == 4
    return jax.shard_map(
        local_fused if one_block else local,
        mesh=mesh,
        in_specs=(
            P(BOTH, None),
            P(BOTH, None),
            P(BOTH, None),
            P(BOTH, None),
            P("expert", "dp"),
            P("expert", "dp"),
            P("expert", "dp"),
        ),
        out_specs=(
            P(BOTH, None),
            P(BOTH, None),
            P("expert", "dp"),
            P("expert", "dp"),
            P("expert", "dp"),
        ),
        check_vma=False,
    )
```

```python
import functools

import jax
import jax.numpy as jnp
import numpy as np
from jax import lax
from jax.experimental import pallas as pl
from jax.experimental.pallas import tpu as pltpu
from jax.sharding import PartitionSpec as P

EXPERTS = 8
CAP = 20
BOTH = ("dp", "expert")
LANES = 128
MESH = pl.DeviceIdType.MESH


def spread(slots, cols, group_size):
    n_dp = lax.axis_size("dp")
    pieces = slots.reshape(EXPERTS, CAP, n_dp, cols).transpose(2, 0, 1, 3)
    sending = jnp.repeat(pieces, group_size, axis=1).reshape(-1, CAP, cols)
    arrived = lax.all_to_all(sending, BOTH, split_axis=0, concat_axis=0, tiled=True)
    return arrived.reshape(-1, cols)


def bring_back(rows, cols, group_size):
    n_dp = lax.axis_size("dp")
    sending = rows.astype(jnp.bfloat16).reshape(-1, CAP, cols)
    arrived = lax.all_to_all(sending, BOTH, split_axis=0, concat_axis=0, tiled=True)
    pieces = arrived.reshape(n_dp, EXPERTS, group_size, CAP, cols)
    if group_size > 1:
        pieces = jnp.sum(pieces.astype(jnp.float32), axis=2).astype(jnp.bfloat16)
    else:
        pieces = pieces[:, :, 0]
    return pieces.transpose(1, 2, 0, 3).reshape(EXPERTS * CAP, n_dp * cols)


def scatter_sum(partial):
    return lax.psum_scatter(
        partial.astype(jnp.bfloat16), "dp", scatter_dimension=0, tiled=True
    ).astype(jnp.float32)


def local(tokens, expert_ids, route_weight, cotangent, w_gate, w_up, w_down):
    cols = w_gate.shape[1]
    group_size = lax.axis_size("expert") // EXPERTS
    chosen = expert_ids[:, 0]
    onehot = (chosen[:, None] == jnp.arange(EXPERTS, dtype=jnp.int32)[None, :]).astype(jnp.int32)
    before = jnp.cumsum(onehot, axis=0) - onehot
    slot_index = chosen * CAP + jnp.sum(before * onehot, axis=1)
    placing = (jnp.arange(EXPERTS * CAP, dtype=jnp.int32)[:, None] == slot_index[None, :]).astype(
        jnp.bfloat16
    )
    scaled = (route_weight * cotangent.astype(jnp.float32)).astype(jnp.bfloat16)
    token_slots = jnp.dot(placing, tokens, preferred_element_type=jnp.float32).astype(jnp.bfloat16)
    grad_slots = jnp.dot(placing, scaled, preferred_element_type=jnp.float32).astype(jnp.bfloat16)
    token_rows = spread(token_slots, cols, group_size)
    gate_pre = scatter_sum(
        jnp.einsum("nd,hd->nh", token_rows, w_gate, preferred_element_type=jnp.float32)
    )
    up_pre = scatter_sum(
        jnp.einsum("nd,hd->nh", token_rows, w_up, preferred_element_type=jnp.float32)
    )
    grad_rows = spread(grad_slots, cols, group_size)
    hidden_grad = scatter_sum(
        jnp.einsum("nd,hd->nh", grad_rows, w_down, preferred_element_type=jnp.float32)
    )
    gate_sigmoid = jax.nn.sigmoid(gate_pre)
    gate_silu = gate_pre * gate_sigmoid
    hidden = (gate_silu * up_pre).astype(jnp.bfloat16)
    hidden = lax.all_gather(hidden, "dp", axis=0, tiled=True)
    gate_grad_pre = (
        hidden_grad * up_pre * (gate_sigmoid * (1.0 + gate_pre * (1.0 - gate_sigmoid)))
    ).astype(jnp.bfloat16)
    gate_grad_pre = lax.all_gather(gate_grad_pre, "dp", axis=0, tiled=True)
    up_grad_pre = (hidden_grad * gate_silu).astype(jnp.bfloat16)
    up_grad_pre = lax.all_gather(up_grad_pre, "dp", axis=0, tiled=True)
    out_slots = bring_back(
        jnp.dot(hidden, w_down, preferred_element_type=jnp.float32), cols, group_size
    )
    input_term = jnp.dot(gate_grad_pre, w_gate, preferred_element_type=jnp.float32) + jnp.dot(
        up_grad_pre, w_up, preferred_element_type=jnp.float32
    )
    back_slots = bring_back(input_term, cols, group_size)
    picked = jnp.einsum("st,sd->td", placing, out_slots, preferred_element_type=jnp.float32)
    layer_out = (route_weight * picked).astype(jnp.bfloat16)
    token_grad = jnp.einsum(
        "st,sd->td", placing, back_slots, preferred_element_type=jnp.float32
    ).astype(jnp.bfloat16)
    gate_grad = jnp.einsum("nh,nd->hd", gate_grad_pre, token_rows, preferred_element_type=jnp.float32)
    up_grad = jnp.einsum("nh,nd->hd", up_grad_pre, token_rows, preferred_element_type=jnp.float32)
    down_grad = jnp.einsum("nh,nd->hd", hidden, grad_rows, preferred_element_type=jnp.float32)
    return (
        layer_out,
        token_grad,
        gate_grad.astype(jnp.bfloat16),
        up_grad.astype(jnp.bfloat16),
        down_grad.astype(jnp.bfloat16),
    )


def dot_nt(a, b):
    return lax.dot_general(a, b, (((1,), (1,)), ((), ())), preferred_element_type=jnp.float32)


def dot_tn(a, b):
    return lax.dot_general(a, b, (((0,), (0,)), ((), ())), preferred_element_type=jnp.float32)


def dot_nn(a, b):
    return jnp.dot(a, b, preferred_element_type=jnp.float32)


def weight_column(row):
    n = row.shape[1]
    same = lax.broadcasted_iota(jnp.int32, (n, n), 0) == lax.broadcasted_iota(jnp.int32, (n, n), 1)
    return jnp.sum(jnp.where(same, row, 0.0), axis=1, keepdims=True)


def fused_kernel(
    n_dp,
    ids_ref,
    weight_ref,
    row_key_ref,
    lane_key_ref,
    tokens_ref,
    cot_ref,
    w_gate_in,
    w_up_in,
    w_down_in,
    final,
    big_t,
    gate_grad_out,
    up_grad_out,
    down_grad_out,
    big,
    w_gate_ref,
    w_up_ref,
    w_down_ref,
    gate_grad_ref,
    up_grad_ref,
    down_grad_ref,
    slots,
    pieces,
    raw,
    rows,
    partial,
    own_partial,
    summed_in,
    relayed,
    hidden_all,
    back_out,
    back_in,
    gather,
    ungather,
    spread_send,
    spread_recv,
    piece_send,
    piece_recv,
    sum_send,
    sum_recv,
    hid_send,
    hid_recv,
    ret_send,
    ret_recv,
    fin_send,
    fin_recv,
    load_sem,
    store_sem,
):
    loads = [
        pltpu.make_async_copy(src, dst, load_sem.at[i])
        for i, (src, dst) in enumerate(
            ((w_gate_in, w_gate_ref), (w_up_in, w_up_ref), (w_down_in, w_down_ref))
        )
    ]
    for cp in loads:
        cp.start()
    n_ex = EXPERTS
    n_tok = tokens_ref.shape[0]
    cols = w_gate_in.shape[1]
    width = w_gate_in.shape[0]
    chunks = cols // LANES
    block = chunks * CAP
    group_rows = n_ex * CAP
    half = group_rows // 2
    d = lax.axis_index("dp")
    e = lax.axis_index("expert")

    across_x = d + 1 - 2 * lax.rem(d, 2)
    peers = (d, across_x, lax.rem(d + 2, 4), 3 - d)

    def dp_at(k):
        return peers[k]

    def ex_at(k):
        return lax.rem(e + k + n_ex, n_ex)

    def copy(src, dst, send_sem, recv_sem, to_dp, to_ex):
        return pltpu.make_async_remote_copy(
            src_ref=src,
            dst_ref=dst,
            send_sem=send_sem,
            recv_sem=recv_sem,
            device_id=(to_dp, to_ex),
            device_id_type=MESH,
        )

    barrier = pltpu.get_barrier_semaphore()
    for k in range(1, n_ex):
        pl.semaphore_signal(barrier, inc=1, device_id=(d, ex_at(k)), device_id_type=MESH)
    for k in range(1, n_dp):
        pl.semaphore_signal(barrier, inc=1, device_id=(dp_at(k), e), device_id_type=MESH)

    ids = ids_ref[...]
    onehot = ids == lax.broadcasted_iota(jnp.int32, (n_ex, n_tok), 0)
    onehot_f = onehot.astype(jnp.float32)
    earlier = (
        lax.broadcasted_iota(jnp.int32, (n_tok, n_tok), 0)
        < lax.broadcasted_iota(jnp.int32, (n_tok, n_tok), 1)
    ).astype(jnp.bfloat16)
    before = dot_nn(onehot_f.astype(jnp.bfloat16), earlier)
    place = jnp.sum(onehot_f * before, axis=0, keepdims=True).astype(jnp.int32)
    slot = ids * CAP + place
    row_key = row_key_ref[...]
    for c in range(chunks):
        big[:, c * n_tok : (c + 1) * n_tok] = (
            (row_key == slot + c * group_rows).astype(jnp.float32).astype(jnp.bfloat16)
        )
    started = []

    def spread(a, source):
        stack = jnp.concatenate(
            [
                jnp.concatenate(
                    [
                        source[:, j * cols + c * LANES : j * cols + (c + 1) * LANES]
                        for j in range(n_dp)
                    ],
                    axis=1,
                )
                for c in range(chunks)
            ],
            axis=0,
        )
        placed = dot_nn(big[...], stack).astype(jnp.bfloat16)
        for j in range(n_dp):
            slots[a, j] = placed[:, j * LANES : (j + 1) * LANES].reshape(n_ex, block, LANES)

    def send_pieces(a):
        for kd in range(1, n_dp):
            to = dp_at(kd)
            cp = copy(
                slots.at[a, to],
                pieces.at[a, kd - 1],
                spread_send.at[a, kd],
                spread_recv.at[a, kd],
                to,
                e,
            )
            cp.start()
            started.append(cp)

    def forward(a, kd):
        if kd > 0:
            dst = pieces.at[a, kd - 1]
            copy(
                dst, dst, spread_send.at[a, kd], spread_recv.at[a, kd], dp_at(kd), e
            ).wait_recv()
            held = pieces.at[a, kd - 1]
        else:
            held = slots.at[a, d]
        for k in range(1, n_ex):
            to = ex_at(k)
            cp = copy(
                held.at[to],
                raw.at[a, kd, e],
                piece_send.at[a, kd, k],
                piece_recv.at[a, kd, k],
                d,
                to,
            )
            cp.start()
            started.append(cp)
        raw[a, kd, e] = held[e]

    spread(0, tokens_ref[...])
    pl.semaphore_wait(barrier, n_ex - 1 + n_dp - 1)
    send_pieces(0)
    forward(0, 0)
    weight = weight_column(weight_ref[...])
    spread(1, (weight * cot_ref[...].astype(jnp.float32)).astype(jnp.bfloat16))
    send_pieces(1)
    lane_key = lane_key_ref[...]
    total_rows = n_ex * block
    want = lax.broadcasted_iota(jnp.int32, (total_rows, 1), 0)
    gather[...] = (lane_key == want).astype(jnp.float32).astype(jnp.bfloat16)
    want = lax.broadcasted_iota(jnp.int32, (1, total_rows), 1)
    ungather[...] = (row_key == want).astype(jnp.float32).astype(jnp.bfloat16)

    big_t[...] = big[...].T
    for cp in loads:
        cp.wait()

    def arrange(a, kd):
        for k in range(1, n_ex):
            source = ex_at(-k)
            dst = raw.at[a, kd, source]
            copy(
                dst, dst, piece_send.at[a, kd, k], piece_recv.at[a, kd, k], d, source
            ).wait_recv()
        arrived = raw[a, kd].reshape(n_ex * block, LANES)
        ordered = dot_nn(gather[...], arrived).astype(jnp.bfloat16)
        for c in range(chunks):
            rows[a, kd, :, c * LANES : (c + 1) * LANES] = ordered[
                c * group_rows : (c + 1) * group_rows
            ]

    upper, lower = pl.ds(0, half), pl.ds(half, half)

    def send_sum(m, i, src, to):
        cp = copy(src, summed_in.at[m, i], sum_send.at[m, i], sum_recv.at[m, i], dp_at(to), e)
        cp.start()
        started.append(cp)

    def wait_sum(m, i, source):
        dst = summed_in.at[m, i]
        copy(dst, dst, sum_send.at[m, i], sum_recv.at[m, i], dp_at(source), e).wait_recv()

    def multiply(m, a, kd, w_ref):
        value = dot_nt(rows[a, kd], w_ref[...])
        if kd == 0:
            own_partial[m] = value
            return
        partial[m, kd - 1] = value.astype(jnp.bfloat16)
        if kd == 1:
            send_sum(m, 0, partial.at[m, 0, upper], 1)
        elif kd == 2:
            send_sum(m, 2, partial.at[m, 1, lower], 2)
        else:
            send_sum(m, 1, partial.at[m, 2, upper], 1)
            send_sum(m, 3, partial.at[m, 2, lower], 2)

    def relay_sum(m):
        wait_sum(m, 1, 1)
        relayed[m, 0] = (
            partial[m, 1, :half].astype(jnp.float32) + summed_in[m, 1].astype(jnp.float32)
        ).astype(jnp.bfloat16)
        send_sum(m, 4, relayed.at[m, 0], 2)
        wait_sum(m, 3, 2)
        relayed[m, 1] = (
            partial[m, 0, half:].astype(jnp.float32) + summed_in[m, 3].astype(jnp.float32)
        ).astype(jnp.bfloat16)
        send_sum(m, 5, relayed.at[m, 1], 1)

    def total(m):
        wait_sum(m, 0, 1)
        wait_sum(m, 2, 2)
        wait_sum(m, 4, 2)
        wait_sum(m, 5, 1)
        own = own_partial[m]
        top = own[:half] + (
            summed_in[m, 0].astype(jnp.float32) + summed_in[m, 4].astype(jnp.float32)
        )
        bottom = own[half:] + (
            summed_in[m, 2].astype(jnp.float32) + summed_in[m, 5].astype(jnp.float32)
        )
        return jnp.concatenate([top, bottom], axis=0)

    forward(0, 1)
    forward(0, 2)
    forward(0, 3)
    forward(1, 0)
    for kd in range(n_dp):
        arrange(0, kd)
        multiply(0, 0, kd, w_gate_ref)
        multiply(1, 0, kd, w_up_ref)
        if kd == 0:
            for other in range(1, n_dp):
                forward(1, other)
    relay_sum(0)
    relay_sum(1)
    for kd in range(n_dp):
        arrange(1, kd)
        multiply(2, 1, kd, w_down_ref)

    def send_hidden(m, kd, src, dst, to):
        cp = copy(src, dst, hid_send.at[m, kd], hid_recv.at[m, kd], dp_at(to), e)
        cp.start()
        started.append(cp)

    def await_hidden(m, kd, dst, source):
        copy(dst, dst, hid_send.at[m, kd], hid_recv.at[m, kd], dp_at(source), e).wait_recv()

    def share(m, value):
        hidden_all[m, 0] = value
        for kd in (1, 2):
            send_hidden(m, kd, hidden_all.at[m, 0], hidden_all.at[m, kd], kd)

    def relay_hidden(m):
        await_hidden(m, 1, hidden_all.at[m, 1], 1)
        send_hidden(m, 3, hidden_all.at[m, 1, lower], hidden_all.at[m, 3, lower], 2)
        await_hidden(m, 2, hidden_all.at[m, 2], 2)
        send_hidden(m, 0, hidden_all.at[m, 2, upper], hidden_all.at[m, 3, upper], 1)

    def last_hidden(m):
        await_hidden(m, 3, hidden_all.at[m, 3, lower], 2)
        await_hidden(m, 0, hidden_all.at[m, 3, upper], 1)

    gate_pre = total(0)
    sigmoid = 1.0 / (1.0 + jnp.exp(-gate_pre))
    silu = gate_pre * sigmoid
    own_partial[0] = silu
    up_pre = total(1)
    share(0, (silu * up_pre).astype(jnp.bfloat16))
    own_partial[1] = up_pre * (sigmoid * (1.0 + gate_pre * (1.0 - sigmoid)))
    def send_back(b, kd, value):
        value = value.astype(jnp.bfloat16)
        stack = jnp.concatenate(
            [value[:, c * LANES : (c + 1) * LANES] for c in range(chunks)], axis=0
        )
        back = dot_nn(ungather[...], stack).astype(jnp.bfloat16).reshape(n_ex, block, LANES)
        if kd == 0:
            back_in[b, 0] = back
            return
        back_out[b, kd - 1] = back
        cp = copy(
            back_out.at[b, kd - 1],
            back_in.at[b, kd],
            ret_send.at[b, kd],
            ret_recv.at[b, kd],
            dp_at(kd),
            e,
        )
        cp.start()
        started.append(cp)

    def finish_send(b, kd):
        if kd > 0:
            copy(
                back_in.at[b, kd],
                back_in.at[b, kd],
                ret_send.at[b, kd],
                ret_recv.at[b, kd],
                dp_at(kd),
                e,
            ).wait_recv()
        j = dp_at(kd)
        for k in range(1, n_ex):
            to = ex_at(k)
            cp = copy(
                back_in.at[b, kd, to],
                final.at[b, j, e],
                fin_send.at[b, kd, k],
                fin_recv.at[b, kd, k],
                d,
                to,
            )
            cp.start()
            started.append(cp)
        final[b, j, e] = back_in[b, kd, e]

    def output(kd):
        send_back(0, kd, dot_nn(hidden_all[0, kd], w_down_ref[...]))

    def input_grad(kd):
        send_back(
            1,
            kd,
            dot_nn(hidden_all[1, kd], w_gate_ref[...]) + dot_nn(hidden_all[2, kd], w_up_ref[...]),
        )

    tile = 256 if width % 256 == 0 else width

    stores = []

    def weight_grad(m, a, out_ref, hbm_ref):
        right = rows[a].reshape(n_dp * group_rows, cols)
        for t in range(width // tile):
            left = hidden_all[m, :, :, t * tile : (t + 1) * tile].reshape(n_dp * group_rows, tile)
            out_ref[t * tile : (t + 1) * tile, :] = dot_tn(left, right).astype(jnp.bfloat16)
        cp = pltpu.make_async_copy(out_ref, hbm_ref, store_sem.at[m])
        cp.start()
        stores.append(cp)

    relay_sum(2)
    output(0)
    finish_send(0, 0)
    relay_hidden(0)
    output(1)
    output(2)
    hidden_grad = total(2)
    share(1, (hidden_grad * own_partial[1]).astype(jnp.bfloat16))
    share(2, (hidden_grad * own_partial[0]).astype(jnp.bfloat16))
    last_hidden(0)
    output(3)
    finish_send(0, 1)
    finish_send(0, 2)
    relay_hidden(1)
    relay_hidden(2)
    input_grad(0)
    finish_send(1, 0)
    finish_send(0, 3)
    input_grad(1)
    input_grad(2)
    last_hidden(1)
    last_hidden(2)
    input_grad(3)
    finish_send(1, 1)
    finish_send(1, 2)
    weight_grad(0, 1, down_grad_ref, down_grad_out)
    finish_send(1, 3)
    weight_grad(1, 0, gate_grad_ref, gate_grad_out)
    weight_grad(2, 0, up_grad_ref, up_grad_out)

    for b in range(2):
        for kd in range(n_dp):
            for k in range(1, n_ex):
                source = ex_at(-k)
                copy(
                    final.at[b, dp_at(kd), source],
                    final.at[b, dp_at(kd), source],
                    fin_send.at[b, kd, k],
                    fin_recv.at[b, kd, k],
                    d,
                    source,
                ).wait_recv()
    for cp in started:
        cp.wait_send()
    for cp in stores:
        cp.wait()


def finish_kernel(
    weight_ref,
    big_ref,
    final_ref,
    gate_in,
    up_in,
    down_in,
    layer_out_ref,
    token_grad_ref,
    gate_out,
    up_out,
    down_out,
    held,
    in_sems,
    out_sems,
):
    loads = [
        pltpu.make_async_copy(src, held.at[i], in_sems.at[i])
        for i, src in enumerate((gate_in, up_in, down_in))
    ]
    stores = [
        pltpu.make_async_copy(held.at[i], dst, out_sems.at[i])
        for i, dst in enumerate((gate_out, up_out, down_out))
    ]
    for cp in loads:
        cp.start()
    n_tok = weight_ref.shape[1]
    n_dp = final_ref.shape[1]
    chunks = big_ref.shape[0] // n_tok
    cols = chunks * LANES
    weight = weight_column(weight_ref[...])
    for b, out_ref in ((0, layer_out_ref), (1, token_grad_ref)):
        slots = jnp.concatenate(
            [final_ref[b, j].reshape(big_ref.shape[1], LANES) for j in range(n_dp)], axis=1
        )
        value = dot_nn(big_ref[...], slots)
        for c in range(chunks):
            piece = value[c * n_tok : (c + 1) * n_tok]
            if b == 0:
                piece = weight * piece
            piece = piece.astype(jnp.bfloat16)
            for j in range(n_dp):
                out_ref[:, j * cols + c * LANES : j * cols + (c + 1) * LANES] = piece[
                    :, j * LANES : (j + 1) * LANES
                ]
        if b == 0:
            for load, store in zip(loads, stores):
                load.wait()
                store.start()
    for cp in stores:
        cp.wait()


def local_fused(tokens, expert_ids, route_weight, cotangent, w_gate, w_up, w_down):
    n_dp = lax.axis_size("dp")
    n_ex = lax.axis_size("expert")
    n_tok, features = tokens.shape
    width, cols = w_gate.shape
    chunks = cols // LANES
    block = chunks * CAP
    group_rows = n_ex * CAP
    at = np.arange(n_ex * block)
    key = (at // block) * CAP + at % CAP + ((at % block) // CAP) * group_rows
    key = key.astype(np.int32)
    bf16 = jnp.bfloat16
    vmem = pl.BlockSpec(memory_space=pltpu.VMEM)
    hbm = pl.BlockSpec(memory_space=pl.ANY)
    dma = pltpu.SemaphoreType.DMA
    weight_row = route_weight.reshape(1, n_tok)
    vmem_limit = 56 * 1024 * 1024
    weight_struct = jax.ShapeDtypeStruct((width, cols), bf16)
    token_struct = jax.ShapeDtypeStruct((n_tok, features), bf16)
    final, big_t, gate_grad, up_grad, down_grad = pl.pallas_call(
        functools.partial(fused_kernel, n_dp),
        out_shape=(
            jax.ShapeDtypeStruct((2, n_dp, n_ex, block, LANES), bf16),
            jax.ShapeDtypeStruct((chunks * n_tok, n_ex * block), bf16),
            weight_struct,
            weight_struct,
            weight_struct,
        ),
        in_specs=[vmem] * 6 + [hbm] * 3,
        out_specs=(vmem,) * 2 + (hbm,) * 3,
        scratch_shapes=[
            pltpu.VMEM((n_ex * block, chunks * n_tok), bf16),
            *[pltpu.VMEM((width, cols), bf16) for _ in range(6)],
            pltpu.VMEM((2, n_dp, n_ex, block, LANES), bf16),
            pltpu.VMEM((2, n_dp - 1, n_ex, block, LANES), bf16),
            pltpu.VMEM((2, n_dp, n_ex, block, LANES), bf16),
            pltpu.VMEM((2, n_dp, group_rows, cols), bf16),
            pltpu.VMEM((3, n_dp - 1, group_rows, width), bf16),
            pltpu.VMEM((3, group_rows, width), jnp.float32),
            pltpu.VMEM((3, 6, group_rows // 2, width), bf16),
            pltpu.VMEM((3, 2, group_rows // 2, width), bf16),
            pltpu.VMEM((3, n_dp, group_rows, width), bf16),
            pltpu.VMEM((2, n_dp - 1, n_ex, block, LANES), bf16),
            pltpu.VMEM((2, n_dp, n_ex, block, LANES), bf16),
            pltpu.VMEM((n_ex * block, n_ex * block), bf16),
            pltpu.VMEM((n_ex * block, n_ex * block), bf16),
            dma((2, n_dp)),
            dma((2, n_dp)),
            dma((2, n_dp, n_ex)),
            dma((2, n_dp, n_ex)),
            dma((3, 6)),
            dma((3, 6)),
            dma((3, n_dp)),
            dma((3, n_dp)),
            dma((2, n_dp)),
            dma((2, n_dp)),
            dma((2, n_dp, n_ex)),
            dma((2, n_dp, n_ex)),
            dma((3,)),
            dma((3,)),
        ],
        compiler_params=pltpu.CompilerParams(
            collective_id=0, has_side_effects=True, vmem_limit_bytes=vmem_limit
        ),
        cost_estimate=pl.CostEstimate(
            flops=18 * n_dp * group_rows * width * cols,
            bytes_accessed=12 * width * cols + 8 * n_tok * features,
            transcendentals=group_rows * width,
        ),
    )(
        expert_ids.reshape(1, n_tok),
        weight_row,
        jnp.asarray(key)[:, None],
        jnp.asarray(key)[None, :],
        tokens,
        cotangent,
        w_gate,
        w_up,
        w_down,
    )
    return pl.pallas_call(
        finish_kernel,
        out_shape=(token_struct, token_struct, weight_struct, weight_struct, weight_struct),
        in_specs=[vmem] * 3 + [hbm] * 3,
        out_specs=(vmem,) * 2 + (hbm,) * 3,
        scratch_shapes=[pltpu.VMEM((3, width, cols), bf16), dma((3,)), dma((3,))],
        compiler_params=pltpu.CompilerParams(vmem_limit_bytes=vmem_limit),
    )(weight_row, big_t, final, gate_grad, up_grad, down_grad)


def solution(mesh):
    one_block = mesh.shape["expert"] == EXPERTS and mesh.shape["dp"] == 4
    return jax.shard_map(
        local_fused if one_block else local,
        mesh=mesh,
        in_specs=(
            P(BOTH, None),
            P(BOTH, None),
            P(BOTH, None),
            P(BOTH, None),
            P("expert", "dp"),
            P("expert", "dp"),
            P("expert", "dp"),
        ),
        out_specs=(
            P(BOTH, None),
            P(BOTH, None),
            P("expert", "dp"),
            P("expert", "dp"),
            P("expert", "dp"),
        ),
        check_vma=False,
    )
```
